32 devices in a mesh: segment: 2 (over core), dp: 8 (over z, x), mp: 2 (over y).
Axes of the slice: x: 2, y: 2, z: 4, core: 2. Of those that a mesh axis runs over, the one named last changes fastest.
Arguments:
- grad_top: bfloat16 [4096, 2048], P('dp'), may hold values from -6 to 6
- saved_query: bfloat16 [2, 4096, 2048], P('segment', 'dp', 'mp'), may hold values from -12 to 12
- saved_key: bfloat16 [2, 6144, 2048], P('segment', 'dp', 'mp'), may hold values from -4 to 4
- saved_value: bfloat16 [2, 6144, 2048], P('segment', 'dp', 'mp'), may hold values from -6 to 6
- w_query: bfloat16 [2, 2048, 2048], P('segment', 'mp', 'dp'), may hold values from -0.125 to 0.125
- w_key: bfloat16 [2, 2048, 2048], P('segment', 'mp', 'dp'), may hold values from -0.125 to 0.125
- w_value: bfloat16 [2, 2048, 2048], P('segment', 'mp', 'dp'), may hold values from -0.125 to 0.125
- w_out: bfloat16 [2, 2048, 2048], P('segment', 'mp', 'dp'), may hold values from -0.125 to 0.125
- query_length: int32 [16, 2], P('dp'), may hold values from 64 to 128
- key_offset: int32 [16, 2], P('dp'), may hold values from 0 to 2, as said below
- key_length: int32 [16, 2], P('dp'), may hold values from 64 to 256
- tile_owner: int32 [16, 3], replicated, may hold values from 0 to 47, as said below
Outputs:
- section_grads: bfloat16 [2, 4096, 2048], P('segment', 'dp', 'mp')
- encoder_grads: bfloat16 [6144, 2048], P('dp', ('segment', 'mp'))
The draws below stay inside these ranges and needn't reach their ends.
Inputs may be any that keep to these rules, and one draw needn't show every extreme that they name: Example 0 takes tiles 0 to key_offset[s, 1] - 1 and example 1 the rest of the sequence's encoder tiles; each example holds at least one tile and its rows fit in its tiles. `tile_owner`: every global tile appears once. Tile t is owned by dp index t // 6; the owner of a tile of dp index i (sequences i * 2 to i * 2 + 1) is i - 1, i or i + 1, wrapping around. Each dp index hands 1 to 2 tiles to each neighbour, and 2 is reached in every draw.
All inputs are finite; a program needn't handle non-finite values.
Results may differ from the reference program's by a relative error of at most 0.019.
Values may be sent and summed in bfloat16 or wider, within the bound.
A program may use at most 128 MiB of HBM per device.

```python
import jax
import jax.numpy as jnp
from jax import lax

D = 2048
HEADS = 8
DH = 256
TILE = 128
NEX = 2
M = 2
CAP = 2
TK = 384
TQ = 256
SEQS = 16
Q_ROWS = 4096
K_ROWS = 6144
N_MP = 2


def packing_table(key):
    base_key = jax.random.fold_in(key, 11)
    first_key, second_key, third_key = jax.random.split(base_key, 3)
    key_tiles = TK // TILE
    first = jax.random.randint(first_key, (SEQS,), 1, key_tiles)
    first = first.at[0].set(key_tiles - 1)
    offsets = jnp.stack([jnp.zeros_like(first), first], axis=1)
    tiles_each = jnp.stack([first, key_tiles - first], axis=1)
    spread = jax.random.randint(second_key, (SEQS, NEX), 0, 1 << 20)
    key_len = TILE // 2 + spread % (tiles_each * TILE - TILE // 2 + 1)
    key_len = key_len.at[0, 0].set((key_tiles - 1) * TILE)
    query_len = jax.random.randint(third_key, (SEQS, NEX), TILE // 2, TILE + 1)
    query_len = query_len.at[0, 0].set(TILE)
    return (offsets.astype(jnp.int32), key_len.astype(jnp.int32), query_len.astype(jnp.int32))


def draw_query_length(key, part):
    return packing_table(key)[2]


def draw_key_offset(key, part):
    return packing_table(key)[0]


def draw_key_length(key, part):
    return packing_table(key)[1]


def draw_tile_owner(key, part):
    base_key = jax.random.fold_in(key, 23)
    send_key, order_key, slot_key = jax.random.split(base_key, 3)
    devices = SEQS // M
    per_device = M * TK // TILE
    sends = jax.random.randint(send_key, (devices,), 1, CAP + 1).at[0].set(CAP)
    previous = jnp.roll(sends, 1)
    order = jax.vmap(lambda sub_key: jax.random.permutation(sub_key, per_device))(jax.random.split(order_key, devices))
    slots = jax.vmap(lambda sub_key: jax.random.permutation(sub_key, per_device))(jax.random.split(slot_key, devices))
    device_ids = jnp.arange(devices, dtype=jnp.int32)[:, None]
    place_ids = jnp.arange(per_device, dtype=jnp.int32)[None, :]
    right_count = sends[:, None]
    left_count = previous[:, None]
    go_right = place_ids < right_count
    go_left = (place_ids >= right_count) & (place_ids < right_count + left_count)
    owner = jnp.where(go_right, (device_ids + 1) % devices, jnp.where(go_left, (device_ids - 1 + devices) % devices, device_ids))
    received_rows = jnp.where(go_right, place_ids, jnp.where(go_left, per_device - left_count + place_ids - right_count, left_count + place_ids - right_count - left_count))
    global_tile = owner * per_device + slots[owner, received_rows]
    inverse = jnp.argsort(order, axis=1)
    dest = jnp.take_along_axis(global_tile, inverse, axis=1)
    return dest.reshape(SEQS, TK // TILE).astype(jnp.int32)


def draw_saved_query(key, part):
    drawn = jax.random.normal(jax.random.fold_in(key, 41), (2, Q_ROWS, HEADS * DH), jnp.float32)
    return jnp.clip(drawn, -4.0, 4.0).astype(jnp.bfloat16)


def draw_saved_key(key, part):
    drawn = jax.random.normal(jax.random.fold_in(key, 43), (2, K_ROWS, HEADS * DH), jnp.float32)
    return jnp.clip(drawn, -4.0, 4.0).astype(jnp.bfloat16)


def steps_of(stream_key, extent, cuts, low, high):
    loudness = 1.0
    for axis_at, blocks in cuts:
        steps = jax.random.uniform(jax.random.fold_in(jax.random.fold_in(stream_key, 6), axis_at), (blocks,), jnp.float32, low / len(cuts), high / len(cuts))
        loudness = loudness * jnp.repeat(jnp.exp(steps), extent[axis_at] // blocks).reshape((-1,) + (1,) * (len(extent) - 1 - axis_at))
    return loudness


def centred(key, extent, scale, reach, pieces=(), held_as=jnp.bfloat16):
    factor_of = steps_of(key, extent, pieces, -0.22, 0.18) if pieces else 1.0
    values = jax.random.normal(key, extent, jnp.float32) * scale * factor_of
    return jnp.minimum(jnp.maximum(values, -reach), reach).astype(held_as)


def setup_inputs(seed: int = 0) -> dict:
    arg_keys = jax.random.split(jax.random.key(seed), 13)
    grad_top = centred(arg_keys[0], (Q_ROWS, D), 1.0, 6.0, ((0, 8),))
    saved_query = draw_saved_query(jax.random.fold_in(arg_keys[12], 71), 0)
    saved_key = draw_saved_key(jax.random.fold_in(arg_keys[12], 71), 0)
    saved_value = centred(arg_keys[3], (2, K_ROWS, HEADS * DH), 1.0, 6.0, ((0, 2), (1, 8), (2, 2)))
    w_query = centred(arg_keys[4], (2, HEADS * DH, D), D ** -0.5, 0.125, ((0, 2), (1, 2), (2, 8)))
    w_key = centred(arg_keys[5], (2, HEADS * DH, D), D ** -0.5, 0.125, ((0, 2), (1, 2), (2, 8)))
    w_value = centred(arg_keys[6], (2, HEADS * DH, D), D ** -0.5, 0.125, ((0, 2), (1, 2), (2, 8)))
    w_out = centred(arg_keys[7], (2, HEADS * DH, D), (HEADS * DH) ** -0.5, 0.125, ((0, 2), (1, 2), (2, 8)))
    query_length = draw_query_length(jax.random.fold_in(arg_keys[12], 71), 0)
    key_offset = draw_key_offset(jax.random.fold_in(arg_keys[12], 71), 0)
    key_length = draw_key_length(jax.random.fold_in(arg_keys[12], 71), 0)
    tile_owner = draw_tile_owner(jax.random.fold_in(arg_keys[12], 71), 0)
    return {"grad_top": grad_top, "saved_query": saved_query, "saved_key": saved_key, "saved_value": saved_value, "w_query": w_query, "w_key": w_key, "w_value": w_value, "w_out": w_out, "query_length": query_length, "key_offset": key_offset, "key_length": key_length, "tile_owner": tile_owner}


masked_floor = -1.0e30


def example_mask(query_length, key_offset, key_length):
    row_ids = jnp.arange(TQ, dtype=jnp.int32)[:, None]
    starts = jnp.arange(NEX, dtype=jnp.int32)[None, :] * TILE
    inside_q = (row_ids >= starts) & (row_ids < starts + query_length[None, :])
    col_ids = jnp.arange(TK, dtype=jnp.int32)[:, None]
    key_start = key_offset[None, :] * TILE
    inside_k = (col_ids >= key_start) & (col_ids < key_start + key_length[None, :])
    return jnp.any(inside_q[:, None, :] & inside_k[None, :, :], axis=-1)


def sequence_backward(grad_in, query_block, key_block, value_block, query_length, key_offset, key_length, w_query, w_out):
    score_scale = DH ** -0.5
    out_grad = jnp.dot(grad_in, w_out.T, preferred_element_type=jnp.float32).astype(jnp.bfloat16)
    q_heads = query_block.reshape(TQ, HEADS, DH).astype(jnp.float32)
    k_heads = key_block.reshape(TK, HEADS, DH).astype(jnp.float32)
    v_heads = value_block.reshape(TK, HEADS, DH).astype(jnp.float32)
    grad_heads = out_grad.reshape(TQ, HEADS, DH).astype(jnp.float32)
    scores = jnp.einsum("qhd,khd->hqk", q_heads, k_heads) * score_scale
    allowed = example_mask(query_length, key_offset, key_length)[None]
    masked = jnp.where(allowed, scores, masked_floor)
    row_max = jnp.max(masked, axis=-1, keepdims=True)
    exp_terms = jnp.where(allowed, jnp.exp(masked - row_max), 0.0)
    denominator = jnp.maximum(jnp.sum(exp_terms, axis=-1, keepdims=True), 1.0)
    attention_probs = exp_terms / denominator
    prob_bf = attention_probs.astype(jnp.bfloat16).astype(jnp.float32)
    attended = jnp.einsum("hqk,khd->qhd", prob_bf, v_heads)
    out_dot = jnp.sum(grad_heads * attended, axis=-1)
    prob_grad = jnp.einsum("qhd,khd->hqk", grad_heads, v_heads)
    score_grad = (attention_probs * (prob_grad - jnp.transpose(out_dot)[:, :, None])).astype(jnp.bfloat16).astype(jnp.float32)
    query_grad = (jnp.einsum("hqk,khd->qhd", score_grad, k_heads) * score_scale).astype(jnp.bfloat16)
    key_gradient = (jnp.einsum("hqk,qhd->khd", score_grad, q_heads) * score_scale).astype(jnp.bfloat16)
    value_grad = jnp.einsum("hqk,qhd->khd", prob_bf, grad_heads).astype(jnp.bfloat16)
    mixed_grad = jnp.dot(query_grad.reshape(TQ, HEADS * DH), w_query, preferred_element_type=jnp.float32)
    section = (grad_in.astype(jnp.float32) + mixed_grad).astype(jnp.bfloat16)
    return section, key_gradient.reshape(TK, HEADS * DH), value_grad.reshape(TK, HEADS * DH)


def layer_backward(grad_rows, query_all, key_all, value_all, w_query, w_out, query_length, key_offset, key_length):
    def one_sequence(items):
        return sequence_backward(items[0], items[1], items[2], items[3], items[4], items[5], items[6], w_query, w_out)

    sections, key_grads, value_grads = lax.map(one_sequence, (
        grad_rows.reshape(SEQS, TQ, D), query_all.reshape(SEQS, TQ, HEADS * DH),
        key_all.reshape(SEQS, TK, HEADS * DH), value_all.reshape(SEQS, TK, HEADS * DH),
        query_length, key_offset, key_length))
    return sections.reshape(Q_ROWS, D), key_grads.reshape(K_ROWS, HEADS * DH), value_grads.reshape(K_ROWS, HEADS * DH)


def group_parts(key_grads, value_grads, w_key, w_value):
    group_width = HEADS * DH // N_MP
    total = jnp.zeros((K_ROWS, D), jnp.float32)
    for group in range(N_MP):
        low = group * group_width
        high = low + group_width
        part_sum = jnp.dot(key_grads[:, low:high], w_key[low:high], preferred_element_type=jnp.float32)
        part_sum = part_sum + jnp.dot(value_grads[:, low:high], w_value[low:high], preferred_element_type=jnp.float32)
        rounded = lax.optimization_barrier(part_sum.astype(jnp.bfloat16))
        total = total + rounded.astype(jnp.float32)
    return total


def reference(grad_top, saved_query, saved_key, saved_value, w_query, w_key, w_value, w_out, query_length, key_offset, key_length, tile_owner):
    upper, key_upper, value_upper = layer_backward(grad_top, saved_query[1], saved_key[1], saved_value[1], w_query[1], w_out[1], query_length, key_offset, key_length)
    lower, key_lower, value_lower = layer_backward(upper, saved_query[0], saved_key[0], saved_value[0], w_query[0], w_out[0], query_length, key_offset, key_length)
    encoder_total = group_parts(key_upper, value_upper, w_key[1], w_value[1])
    encoder_total = encoder_total + group_parts(key_lower, value_lower, w_key[0], w_value[0])
    source_tiles = encoder_total.astype(jnp.bfloat16).reshape(SEQS * (TK // TILE), TILE, D)
    placed_tiles = jnp.zeros_like(source_tiles).at[tile_owner.reshape(-1).astype(jnp.int32)].set(source_tiles)
    return jnp.stack([lower, upper]), placed_tiles.reshape(K_ROWS, D)
```

```python
import jax
import jax.numpy as jnp
from jax import lax
from jax.sharding import PartitionSpec as P

DH = 256
TILE = 128
CAP = 2


masked_floor = -1e30


def shifted(block, axis, distance):
    devices = range(lax.axis_size(axis))
    route = [(i - distance, i) for i in devices if i - distance in devices]
    return lax.ppermute(block, axis, route)


def extended_2(block, sides, width):
    for axis, dim in sides:
        count = lax.axis_size(axis)
        forward = [(i, i + 1) for i in range(count - 1)]
        forward.append((count - 1, 0))
        backward = [(target, source) for source, target in forward]
        low = lax.ppermute(
            lax.slice_in_dim(block, block.shape[dim] - width, None, axis=dim), axis, forward
        )
        high = lax.ppermute(lax.slice_in_dim(block, 0, width, axis=dim), axis, backward)
        block = jnp.concatenate([low, block, high], axis=dim)
    return block


def example_mask(query_length, key_offset, key_length, q_rows, k_rows):
    row_ids = jnp.arange(q_rows, dtype=jnp.int32)[:, None]
    starts = jnp.arange(query_length.shape[0], dtype=jnp.int32)[None, :] * TILE
    inside_q = (row_ids >= starts) & (row_ids < starts + query_length[None, :])
    col_ids = jnp.arange(k_rows, dtype=jnp.int32)[:, None]
    key_start = key_offset[None, :] * TILE
    inside_k = (col_ids >= key_start) & (col_ids < key_start + key_length[None, :])
    return jnp.any(inside_q[:, None, :] & inside_k[None, :, :], axis=-1)


def sequence_backward(operands, query_full, out_full):
    grad_in, query_block, key_block, value_block, query_length, key_offset, key_length = operands
    q_rows, local_width = query_block.shape
    k_rows = key_block.shape[0]
    head_count = local_width // DH
    score_scale = DH ** (-0.5)
    out_grad = lax.dot_general(
        grad_in, out_full, (((1,), (1,)), ((), ())), preferred_element_type=jnp.float32
    ).astype(jnp.bfloat16)
    q_heads = query_block.reshape(q_rows, head_count, DH)
    k_heads = key_block.reshape(k_rows, head_count, DH)
    v_heads = value_block.reshape(k_rows, head_count, DH)
    grad_heads = out_grad.reshape(q_rows, head_count, DH)
    scores = (
        jnp.einsum("qhd,khd->hqk", q_heads, k_heads, preferred_element_type=jnp.float32)
        * score_scale
    )
    allowed = example_mask(query_length, key_offset, key_length, q_rows, k_rows)[None]
    masked = jnp.where(allowed, scores, masked_floor)
    row_max = jnp.max(masked, axis=-1, keepdims=True)
    exp_terms = jnp.where(allowed, jnp.exp(masked - row_max), 0.0)
    denominator = jnp.maximum(jnp.sum(exp_terms, axis=-1, keepdims=True), 1.0)
    attention_probs = exp_terms / denominator
    prob_bf = attention_probs.astype(jnp.bfloat16)
    attended = jnp.einsum("hqk,khd->qhd", prob_bf, v_heads, preferred_element_type=jnp.float32)
    out_dot = jnp.sum(grad_heads.astype(jnp.float32) * attended, axis=-1)
    prob_grad = jnp.einsum("qhd,khd->hqk", grad_heads, v_heads, preferred_element_type=jnp.float32)
    score_grad = (attention_probs * (prob_grad - jnp.transpose(out_dot)[:, :, None])).astype(
        jnp.bfloat16
    )
    query_grad = (
        jnp.einsum("hqk,khd->qhd", score_grad, k_heads, preferred_element_type=jnp.float32)
        * score_scale
    ).astype(jnp.bfloat16)
    key_gradient = (
        jnp.einsum("hqk,qhd->khd", score_grad, q_heads, preferred_element_type=jnp.float32)
        * score_scale
    ).astype(jnp.bfloat16)
    value_grad = jnp.einsum(
        "hqk,qhd->khd", prob_bf, grad_heads, preferred_element_type=jnp.float32
    ).astype(jnp.bfloat16)
    mixed_grad = jnp.dot(
        query_grad.reshape(q_rows, local_width), query_full, preferred_element_type=jnp.float32
    )
    return (
        mixed_grad,
        key_gradient.reshape(k_rows, local_width),
        value_grad.reshape(k_rows, local_width),
    )


def ranked(marked):
    ids = jnp.arange(marked.shape[0], dtype=jnp.int32)
    upto = ids[None, :] <= ids[:, None]
    return jnp.sum((upto & marked[None, :]).astype(jnp.int32), axis=1) - 1


def on_device(
    grad_top,
    saved_query,
    saved_key,
    saved_value,
    w_query,
    w_key,
    w_value,
    w_out,
    query_length,
    key_offset,
    key_length,
    tile_owner,
):
    segment_count = lax.axis_size("segment")
    segment_id = lax.axis_index("segment")
    micro_count = query_length.shape[0]
    q_rows = grad_top.shape[0] // micro_count
    k_rows = saved_key.shape[1] // micro_count
    width = grad_top.shape[1]
    local_width = saved_query.shape[2]
    half_width = width // lax.axis_size("mp")
    out_full, query_full, key_full, complete_value = (
        lax.all_gather(w_out[0], "dp", axis=1, tiled=True),
        lax.all_gather(w_query[0], "dp", axis=1, tiled=True),
        lax.all_gather(w_key[0], "dp", axis=1, tiled=True),
        lax.all_gather(w_value[0], "dp", axis=1, tiled=True),
    )

    def run_layer(operands):
        return sequence_backward(operands, query_full, out_full)

    def bypass_layer(operands):
        return (
            jnp.zeros((q_rows, width), jnp.float32),
            jnp.zeros((k_rows, local_width), jnp.bfloat16),
            jnp.zeros((k_rows, local_width), jnp.bfloat16),
        )

    incoming = jnp.zeros((q_rows, width), jnp.bfloat16)
    sections = jnp.zeros((micro_count * q_rows, half_width), jnp.bfloat16)
    key_grads = jnp.zeros((micro_count * k_rows, local_width), jnp.bfloat16)
    value_grads = jnp.zeros((micro_count * k_rows, local_width), jnp.bfloat16)
    for clock_tick in range(micro_count + 1):
        step_id = clock_tick - 1 + segment_id
        active = (step_id >= 0) & (step_id < micro_count)
        picked = jnp.clip(step_id, 0, micro_count - 1)
        top_rows = lax.dynamic_slice_in_dim(grad_top, picked * q_rows, q_rows, 0)
        grad_in = jnp.where(segment_id == segment_count - 1, top_rows, incoming)
        query_block = lax.dynamic_slice_in_dim(saved_query[0], picked * q_rows, q_rows, 0)
        key_block = lax.dynamic_slice_in_dim(saved_key[0], picked * k_rows, k_rows, 0)
        value_block = lax.dynamic_slice_in_dim(saved_value[0], picked * k_rows, k_rows, 0)
        lengths_q = lax.dynamic_index_in_dim(query_length, picked, 0, keepdims=False)
        offsets_k = lax.dynamic_index_in_dim(key_offset, picked, 0, keepdims=False)
        lengths_k = lax.dynamic_index_in_dim(key_length, picked, 0, keepdims=False)
        mixed_grad, key_gradient, value_grad = lax.cond(
            active,
            run_layer,
            bypass_layer,
            (grad_in, query_block, key_block, value_block, lengths_q, offsets_k, lengths_k),
        )
        summed_share = lax.psum_scatter(
            mixed_grad.astype(jnp.bfloat16), "mp", scatter_dimension=1, tiled=True
        ).astype(jnp.float32)
        own_input = lax.dynamic_slice_in_dim(
            grad_in, lax.axis_index("mp") * half_width, half_width, 1
        )
        own_section = (own_input.astype(jnp.float32) + summed_share).astype(jnp.bfloat16)
        if clock_tick < micro_count:
            full_section = lax.all_gather(own_section, "mp", axis=1, tiled=True)
        sections = jnp.where(
            active,
            lax.dynamic_update_slice_in_dim(sections, own_section, picked * q_rows, 0),
            sections,
        )
        key_grads = jnp.where(
            active,
            lax.dynamic_update_slice_in_dim(key_grads, key_gradient, picked * k_rows, 0),
            key_grads,
        )
        value_grads = jnp.where(
            active,
            lax.dynamic_update_slice_in_dim(value_grads, value_grad, picked * k_rows, 0),
            value_grads,
        )
        if clock_tick < micro_count:
            incoming = shifted(full_section, "segment", -1)
    encoder_partial = jnp.dot(key_grads, key_full, preferred_element_type=jnp.float32) + jnp.dot(
        value_grads, complete_value, preferred_element_type=jnp.float32
    )
    reduced = lax.psum_scatter(
        encoder_partial.astype(jnp.bfloat16), ("segment", "mp"), scatter_dimension=1, tiled=True
    )
    tiles_dev = reduced.shape[0] // TILE
    features = reduced.shape[1]
    local_tiles = reduced.reshape(tiles_dev, TILE, features)
    devices = lax.axis_size("dp")
    my_index = lax.axis_index("dp")
    owners_all = tile_owner.reshape(devices, tiles_dev)

    def route_plan(source):
        owner_row = lax.dynamic_index_in_dim(owners_all, source % devices, 0, keepdims=False)
        owner_step = (owner_row // tiles_dev - source % devices + devices) % devices
        return (owner_step, owner_row % tiles_dev)

    mine_step, mine_slot = route_plan(my_index)
    left_step, left_slot = route_plan(my_index - 1 + devices)
    right_step, right_slot = route_plan(my_index + 1)
    capacity_ids = jnp.arange(CAP, dtype=jnp.int32)[:, None]
    to_left = mine_step == devices - 1
    rightward_send = mine_step == 1
    pick_left = (ranked(to_left)[None, :] == capacity_ids) & to_left[None, :]
    pick_right = (ranked(rightward_send)[None, :] == capacity_ids) & rightward_send[None, :]
    selector_mask = jnp.concatenate([pick_left, pick_right], axis=0).astype(jnp.bfloat16)
    outgoing = jnp.einsum(
        "sa,ayk->syk", selector_mask, local_tiles, preferred_element_type=jnp.float32
    ).astype(jnp.bfloat16)
    outgoing = outgoing.reshape(2 * CAP * TILE, features)
    extended = extended_2(outgoing, (("dp", 0),), CAP * TILE)
    from_left = extended[: CAP * TILE].reshape(CAP, TILE, features)
    from_right = extended[extended.shape[0] - CAP * TILE :].reshape(CAP, TILE, features)
    candidates = jnp.concatenate([from_left, local_tiles, from_right], axis=0)
    left_marked = left_step == 1
    left_hit = (ranked(left_marked)[None, :] == capacity_ids) & left_marked[None, :]
    left_target = jnp.sum(jnp.where(left_hit, left_slot[None, :], 0), axis=1)
    right_marked = right_step == devices - 1
    right_hit = (ranked(right_marked)[None, :] == capacity_ids) & right_marked[None, :]
    right_target = jnp.sum(jnp.where(right_hit, right_slot[None, :], 0), axis=1)
    target = jnp.concatenate([left_target, mine_slot, right_target])
    usable = jnp.concatenate(
        [jnp.any(left_hit, axis=1), mine_step == 0, jnp.any(right_hit, axis=1)]
    )
    placer = (
        (jnp.arange(tiles_dev, dtype=jnp.int32)[:, None] == target[None, :]) & usable[None, :]
    ).astype(jnp.bfloat16)
    owned_rows = jnp.einsum(
        "sc,crf->srf", placer, candidates, preferred_element_type=jnp.float32
    ).astype(jnp.bfloat16)
    return (sections[None], owned_rows.reshape(tiles_dev * TILE, features))


def solution(mesh):
    in_specs = (
        P("dp", None),
        P("segment", "dp", "mp"),
        P("segment", "dp", "mp"),
        P("segment", "dp", "mp"),
        P("segment", "mp", "dp"),
        P("segment", "mp", "dp"),
        P("segment", "mp", "dp"),
        P("segment", "mp", "dp"),
        P("dp", None),
        P("dp", None),
        P("dp", None),
        P(),
    )
    out_specs = (P("segment", "dp", "mp"), P("dp", ("segment", "mp")))
    return jax.shard_map(
        on_device, mesh=mesh, in_specs=in_specs, out_specs=out_specs, check_vma=False
    )
```

```python
import functools

import jax
import jax.numpy as jnp
from jax import lax
from jax.experimental import pallas as pl
from jax.experimental.pallas import tpu as pltpu
from jax.sharding import PartitionSpec as P

DH = 256
TILE = 128
CAP = 2
BLOCK = 256
masked_floor = -1e30
BF16, F32 = jnp.bfloat16, jnp.float32


def dot(a, b, ca, cb):
    return lax.dot_general(a, b, (((ca,), (cb,)), ((), ())), preferred_element_type=F32)


def tick_kernel(count, half, sc, g_ref, q_ref, k_ref, v_ref, *rest):
    wo, wq = rest[:count], rest[count : 2 * count]
    mixed_ref, kg_ref, vg_ref, acc = rest[2 * count :]
    head = pl.program_id(0)
    per = half // BLOCK
    scale = DH ** (-0.5)

    def place(b):
        src = sc[b]
        return src // per, pl.ds(pl.multiple_of((src % per) * BLOCK, BLOCK), BLOCK)

    og = None
    for b in range(count):
        at, cols = place(b)
        term = dot(g_ref[at, :, cols], wo[b][...], 1, 1)
        og = term if og is None else og + term
    og = og.astype(BF16)
    q, k, v = q_ref[0], k_ref[0], v_ref[0]
    scores = dot(q, k, 1, 1) * scale
    rows = lax.broadcasted_iota(jnp.int32, scores.shape, 0)
    cols_id = lax.broadcasted_iota(jnp.int32, scores.shape, 1)
    allowed = None
    for e in range(2):
        q_len, k_off, k_len = sc[count + e], sc[count + 2 + e] * TILE, sc[count + 4 + e]
        hit = (rows >= e * TILE) & (rows < e * TILE + q_len)
        hit = hit & (cols_id >= k_off) & (cols_id < k_off + k_len)
        allowed = hit if allowed is None else allowed | hit
    masked = jnp.where(allowed, scores, masked_floor)
    top = jnp.max(masked, axis=-1, keepdims=True)
    terms = jnp.where(allowed, jnp.exp(masked - top), 0.0)
    prob = terms / jnp.maximum(jnp.sum(terms, axis=-1, keepdims=True), 1.0)
    prob_bf = prob.astype(BF16)
    attended = dot(prob_bf, v, 1, 0)
    out_dot = jnp.sum(og.astype(F32) * attended, axis=-1, keepdims=True)
    sg = (prob * (dot(og, v, 1, 1) - out_dot)).astype(BF16)
    qg = (dot(sg, k, 1, 0) * scale).astype(BF16)
    kg_ref[...] = (dot(sg, q, 0, 0) * scale).astype(BF16)
    vg_ref[...] = dot(prob_bf, og, 0, 0).astype(BF16)

    @pl.when(head == 0)
    def _():
        acc[...] = jnp.zeros_like(acc)

    for b in range(count):
        at, cols = place(b)
        acc[at, :, cols] += dot(qg, wq[b][...], 1, 0)

    @pl.when(head == pl.num_programs(0) - 1)
    def _():
        mixed_ref[...] = acc[...].astype(BF16)


def run_tick(scalars, grad, at, seq, saved_q, saved_k, saved_v, wo, wq, q_rows, k_rows):
    half = grad.shape[2]
    heads = saved_q.shape[2] // DH
    count = len(wo)
    weight = pl.BlockSpec((DH, BLOCK), lambda h, sc: (h, 0))
    macs = heads * q_rows * DH * (4 * half + 6 * k_rows)
    return pl.pallas_call(
        functools.partial(tick_kernel, count, half),
        grid_spec=pltpu.PrefetchScalarGridSpec(
            num_scalar_prefetch=1,
            grid=(heads,),
            in_specs=[
                pl.BlockSpec((2, q_rows, half), lambda h, sc: (0, at, 0)),
                pl.BlockSpec((1, q_rows, DH), lambda h, sc: (0, seq, h)),
                pl.BlockSpec((1, k_rows, DH), lambda h, sc: (0, seq, h)),
                pl.BlockSpec((1, k_rows, DH), lambda h, sc: (0, seq, h)),
            ]
            + [weight] * (2 * count),
            out_specs=[
                pl.BlockSpec((2, q_rows, half), lambda h, sc: (0, 0, 0)),
                pl.BlockSpec((k_rows, DH), lambda h, sc: (0, h)),
                pl.BlockSpec((k_rows, DH), lambda h, sc: (0, h)),
            ],
            scratch_shapes=[pltpu.VMEM((2, q_rows, half), F32)],
        ),
        out_shape=[
            jax.ShapeDtypeStruct((2, q_rows, half), BF16),
            jax.ShapeDtypeStruct((k_rows, heads * DH), BF16),
            jax.ShapeDtypeStruct((k_rows, heads * DH), BF16),
        ],
        compiler_params=pltpu.CompilerParams(vmem_limit_bytes=40 << 20),
        cost_estimate=pl.CostEstimate(
            flops=2 * macs, bytes_accessed=16 << 20, transcendentals=heads * q_rows * k_rows
        ),
    )(scalars, grad, saved_q, saved_k, saved_v, *wo, *wq)


def encoder_kernel(count, quarter, sc, kg_ref, vg_ref, *rest):
    wk, wv, out_ref = rest[:count], rest[count : 2 * count], rest[2 * count]
    per = quarter // BLOCK
    kg, vg = kg_ref[...], vg_ref[...]
    for b in range(count):
        src = sc[b]
        cols = pl.ds(pl.multiple_of((src % per) * BLOCK, BLOCK), BLOCK)
        part = dot(kg, wk[b][...], 1, 0) + dot(vg, wv[b][...], 1, 0)
        out_ref[src // per, :, cols] = part.astype(BF16)


def run_encoder(scalars, kg, vg, wk, wv):
    count = len(wk)
    rows, depth = kg.shape
    quarter = count * BLOCK // 4
    step = 256
    whole = pl.BlockSpec((depth, BLOCK), lambda i, sc: (0, 0))
    return pl.pallas_call(
        functools.partial(encoder_kernel, count, quarter),
        grid_spec=pltpu.PrefetchScalarGridSpec(
            num_scalar_prefetch=1,
            grid=(rows // step,),
            in_specs=[pl.BlockSpec((step, depth), lambda i, sc: (i, 0))] * 2
            + [whole] * (2 * count),
            out_specs=pl.BlockSpec((4, step, quarter), lambda i, sc: (0, i, 0)),
        ),
        out_shape=jax.ShapeDtypeStruct((4, rows, quarter), BF16),
        compiler_params=pltpu.CompilerParams(vmem_limit_bytes=48 << 20),
        cost_estimate=pl.CostEstimate(
            flops=16 * rows * depth * quarter, bytes_accessed=14 << 20, transcendentals=0
        ),
    )(scalars, kg, vg, *wk, *wv)


def pick_kernel(sc, own_ref, other_ref, local_ref, left_ref, right_ref):
    local_ref[...] = (own_ref[...].astype(F32) + other_ref[...].astype(F32)).astype(BF16)
    for c in range(CAP):
        left_ref[c] = local_ref[sc[c]]
        right_ref[c] = local_ref[sc[CAP + c]]


def place_kernel(sc, left_ref, local_ref, right_ref, out_ref):
    tiles = local_ref.shape[0]
    for s in range(tiles):
        i = sc[s]

        @pl.when(i < CAP)
        def _():
            out_ref[s] = left_ref[jnp.minimum(i, CAP - 1)]

        @pl.when((i >= CAP) & (i < CAP + tiles))
        def _():
            out_ref[s] = local_ref[jnp.clip(i - CAP, 0, tiles - 1)]

        @pl.when(i >= CAP + tiles)
        def _():
            out_ref[s] = right_ref[jnp.clip(i - CAP - tiles, 0, CAP - 1)]


def small_call(body, scalars, arrays, outs):
    vmem = pl.BlockSpec(memory_space=pltpu.VMEM)
    single = not isinstance(outs, list)
    return pl.pallas_call(
        body,
        in_specs=[pl.BlockSpec(memory_space=pltpu.SMEM)] + [vmem] * len(arrays),
        out_specs=vmem if single else [vmem] * len(outs),
        out_shape=outs,
        compiler_params=pltpu.CompilerParams(vmem_limit_bytes=24 << 20),
    )(scalars, *arrays)


def gathered(shard, factors):
    count = lax.axis_size("dp")
    me = lax.axis_index("dp")
    if shard.shape[1] != BLOCK or factors is None:
        full = lax.all_gather(shard, "dp", axis=1, tiled=True)
        blocks = [full[:, i : i + BLOCK] for i in range(0, full.shape[1], BLOCK)]
        return blocks, list(jnp.arange(len(blocks), dtype=jnp.int32))
    outer, inner = factors
    ring = [(i, (i + inner) % count) for i in range(count)]
    swap = [(i, i ^ 1) for i in range(count)]
    blocks, sources = [], []
    block = shard
    for r in range(outer):
        if r:
            block = lax.ppermute(block, "dp", ring)
        source = (me - r * inner + count) % count
        blocks.append(block)
        sources.append(source)
        blocks.append(lax.ppermute(block, "dp", swap))
        sources.append(source ^ 1)
    return blocks, sources


def ranked(marked):
    ids = jnp.arange(marked.shape[0], dtype=jnp.int32)
    upto = ids[None, :] <= ids[:, None]
    return jnp.sum((upto & marked[None, :]).astype(jnp.int32), axis=1) - 1


def on_device(
    grad_top,
    saved_query,
    saved_key,
    saved_value,
    w_query,
    w_key,
    w_value,
    w_out,
    query_length,
    key_offset,
    key_length,
    tile_owner,
):
    seg = lax.axis_index("segment")
    mp = lax.axis_index("mp")
    devices = lax.axis_size("dp")
    me = lax.axis_index("dp")
    micro = query_length.shape[0]
    q_rows = grad_top.shape[0] // micro
    k_rows = saved_key.shape[1] // micro
    half = grad_top.shape[1] // 2
    factors = (devices // 2, 2) if devices % 2 == 0 else None
    wo, sources = gathered(w_out[0], factors)
    wq, _ = gathered(w_query[0], factors)
    wk, _ = gathered(w_key[0], factors)
    wv, _ = gathered(w_value[0], factors)
    order = jnp.stack(sources).astype(jnp.int32)

    mp_swap = [(0, 1), (1, 0)]
    top = grad_top.reshape(grad_top.shape[0], 2, half).transpose(1, 0, 2)
    scalars = [
        jnp.concatenate([order, query_length[s], key_offset[s], key_length[s]])
        for s in range(micro)
    ]

    def tick(s, grad, at):
        return run_tick(
            scalars[s], grad, at, s, saved_query, saved_key, saved_value, wo, wq, q_rows, k_rows
        )

    upper = [tick(s, top, s) for s in range(micro)]
    upper_half, incoming = [], []
    for s in range(micro):
        mixed = upper[s][0]
        other = lax.ppermute(mixed, "mp", mp_swap)
        rows = top[:, s * q_rows : (s + 1) * q_rows]
        section = (rows.astype(F32) + (mixed.astype(F32) + other.astype(F32))).astype(BF16)
        incoming.append(lax.ppermute(section, "segment", [(1, 0)]))
        upper_half.append(lax.dynamic_index_in_dim(section, mp, 0, keepdims=False))
    lower = [tick(s, incoming[s], 0) for s in range(micro)]
    halves = []
    for s in range(micro):
        mixed = lower[s][0]
        other = lax.ppermute(
            lax.dynamic_index_in_dim(mixed, 1 - mp, 0, keepdims=False), "mp", mp_swap
        )
        own = lax.dynamic_index_in_dim(mixed, mp, 0, keepdims=False)
        base = lax.dynamic_index_in_dim(incoming[s], mp, 0, keepdims=False)
        low = (base.astype(F32) + (own.astype(F32) + other.astype(F32))).astype(BF16)
        halves.append(jnp.where(seg == 1, upper_half[s], low))
    sections = jnp.concatenate(halves, axis=0)

    kg = jnp.concatenate([jnp.where(seg == 1, upper[s][1], lower[s][1]) for s in range(micro)], 0)
    vg = jnp.concatenate([jnp.where(seg == 1, upper[s][2], lower[s][2]) for s in range(micro)], 0)
    parts = run_encoder(order, kg, vg, wk, wv)
    away = lax.dynamic_slice_in_dim(parts, (1 - seg) * 2, 2, 0)
    mine = lax.dynamic_slice_in_dim(parts, seg * 2, 2, 0)
    arrived = lax.ppermute(away, "segment", mp_swap)
    summed = (mine.astype(F32) + arrived.astype(F32)).astype(BF16)
    crossing = lax.ppermute(
        lax.dynamic_index_in_dim(summed, 1 - mp, 0, keepdims=False), "mp", mp_swap
    )
    kept = lax.dynamic_index_in_dim(summed, mp, 0, keepdims=False)

    tiles = kept.shape[0] // TILE
    features = kept.shape[1]
    owners = tile_owner.reshape(devices, tiles)
    slot_ids = jnp.arange(CAP, dtype=jnp.int32)[:, None]
    tile_ids = jnp.arange(tiles, dtype=jnp.int32)

    def plan(source):
        source = source % devices
        row = lax.dynamic_index_in_dim(owners, source, 0, keepdims=False)
        return (row // tiles - source + devices) % devices, row % tiles

    def ranks_of(marked):
        return (ranked(marked)[None, :] == slot_ids) & marked[None, :]

    step, slot = plan(me)
    left_step, left_slot = plan(me - 1 + devices)
    right_step, right_slot = plan(me + 1)
    send_left = jnp.sum(jnp.where(ranks_of(step == devices - 1), tile_ids[None, :], 0), axis=1)
    send_right = jnp.sum(jnp.where(ranks_of(step == 1), tile_ids[None, :], 0), axis=1)
    left_hit = ranks_of(left_step == 1)
    right_hit = ranks_of(right_step == devices - 1)
    target = jnp.concatenate(
        [
            jnp.sum(jnp.where(left_hit, left_slot[None, :], 0), axis=1),
            slot,
            jnp.sum(jnp.where(right_hit, right_slot[None, :], 0), axis=1),
        ]
    )
    usable = jnp.concatenate([jnp.any(left_hit, axis=1), step == 0, jnp.any(right_hit, axis=1)])
    chosen = (tile_ids[:, None] == target[None, :]) & usable[None, :]
    candidate_ids = jnp.arange(target.shape[0], dtype=jnp.int32)
    take = jnp.sum(jnp.where(chosen, candidate_ids[None, :], 0), axis=1)

    tiled = (tiles, TILE, features)
    shape = jax.ShapeDtypeStruct(tiled, BF16)
    handed = jax.ShapeDtypeStruct((CAP, TILE, features), BF16)
    local, to_left, to_right = small_call(
        pick_kernel,
        jnp.concatenate([send_left, send_right]),
        [kept.reshape(tiled), crossing.reshape(tiled)],
        [shape, handed, handed],
    )
    forward = [(i, (i + 1) % devices) for i in range(devices)]
    backward = [(b, a) for a, b in forward]
    from_left = lax.ppermute(to_right, "dp", forward)
    from_right = lax.ppermute(to_left, "dp", backward)
    owned = small_call(place_kernel, take, [from_left, local, from_right], shape)
    return sections[None], owned.reshape(tiles * TILE, features)


def solution(mesh):
    in_specs = (
        P("dp", None),
        P("segment", "dp", "mp"),
        P("segment", "dp", "mp"),
        P("segment", "dp", "mp"),
        P("segment", "mp", "dp"),
        P("segment", "mp", "dp"),
        P("segment", "mp", "dp"),
        P("segment", "mp", "dp"),
        P("dp", None),
        P("dp", None),
        P("dp", None),
        P(),
    )
    out_specs = (P("segment", "dp", "mp"), P("dp", ("segment", "mp")))
    return jax.shard_map(
        on_device, mesh=mesh, in_specs=in_specs, out_specs=out_specs, check_vma=False
    )
```

```python
import functools

import jax
import jax.numpy as jnp
from jax import lax
from jax.experimental import pallas as pl
from jax.experimental.pallas import tpu as pltpu
from jax.sharding import PartitionSpec as P

DH = 256
TILE = 128
CAP = 2
BLOCK = 256
masked_floor = -1e30
BF16, F32 = jnp.bfloat16, jnp.float32


def dot(a, b, ca, cb):
    return lax.dot_general(a, b, (((ca,), (cb,)), ((), ())), preferred_element_type=F32)


def tick_kernel(count, half, sc, g_ref, q_ref, k_ref, v_ref, *rest):
    wo, wq = rest[:count], rest[count : 2 * count]
    mixed_ref, kg_ref, vg_ref, acc = rest[2 * count :]
    head = pl.program_id(0)
    per = half // BLOCK
    scale = DH ** (-0.5)

    def place(b):
        src = sc[b]
        return src // per, pl.ds(pl.multiple_of((src % per) * BLOCK, BLOCK), BLOCK)

    og = None
    for b in range(count):
        at, cols = place(b)
        term = dot(g_ref[at, :, cols], wo[b][...], 1, 1)
        og = term if og is None else og + term
    og = og.astype(BF16)
    q, k, v = q_ref[0], k_ref[0], v_ref[0]
    scores = dot(q, k, 1, 1) * scale
    rows = lax.broadcasted_iota(jnp.int32, scores.shape, 0)
    cols_id = lax.broadcasted_iota(jnp.int32, scores.shape, 1)
    allowed = None
    for e in range(2):
        q_len, k_off, k_len = sc[count + e], sc[count + 2 + e] * TILE, sc[count + 4 + e]
        hit = (rows >= e * TILE) & (rows < e * TILE + q_len)
        hit = hit & (cols_id >= k_off) & (cols_id < k_off + k_len)
        allowed = hit if allowed is None else allowed | hit
    masked = jnp.where(allowed, scores, masked_floor)
    top = jnp.max(masked, axis=-1, keepdims=True)
    terms = jnp.where(allowed, jnp.exp(masked - top), 0.0)
    prob = terms / jnp.maximum(jnp.sum(terms, axis=-1, keepdims=True), 1.0)
    prob_bf = prob.astype(BF16)
    attended = dot(prob_bf, v, 1, 0)
    out_dot = jnp.sum(og.astype(F32) * attended, axis=-1, keepdims=True)
    sg = (prob * (dot(og, v, 1, 1) - out_dot)).astype(BF16)
    qg = (dot(sg, k, 1, 0) * scale).astype(BF16)
    kg_ref[...] = (dot(sg, q, 0, 0) * scale).astype(BF16)
    vg_ref[...] = dot(prob_bf, og, 0, 0).astype(BF16)

    @pl.when(head == 0)
    def _():
        acc[...] = jnp.zeros_like(acc)

    for b in range(count):
        at, cols = place(b)
        acc[at, :, cols] += dot(qg, wq[b][...], 1, 0)

    @pl.when(head == pl.num_programs(0) - 1)
    def _():
        mixed_ref[...] = acc[...].astype(BF16)


def run_tick(scalars, grad, at, seq, saved_q, saved_k, saved_v, wo, wq, q_rows, k_rows):
    half = grad.shape[2]
    heads = saved_q.shape[2] // DH
    count = len(wo)
    weight = pl.BlockSpec((DH, BLOCK), lambda h, sc: (h, 0))
    macs = heads * q_rows * DH * (4 * half + 6 * k_rows)
    return pl.pallas_call(
        functools.partial(tick_kernel, count, half),
        grid_spec=pltpu.PrefetchScalarGridSpec(
            num_scalar_prefetch=1,
            grid=(heads,),
            in_specs=[
                pl.BlockSpec((2, q_rows, half), lambda h, sc: (0, at, 0)),
                pl.BlockSpec((1, q_rows, DH), lambda h, sc: (0, seq, h)),
                pl.BlockSpec((1, k_rows, DH), lambda h, sc: (0, seq, h)),
                pl.BlockSpec((1, k_rows, DH), lambda h, sc: (0, seq, h)),
            ]
            + [weight] * (2 * count),
            out_specs=[
                pl.BlockSpec((2, q_rows, half), lambda h, sc: (0, 0, 0)),
                pl.BlockSpec((k_rows, DH), lambda h, sc: (0, h)),
                pl.BlockSpec((k_rows, DH), lambda h, sc: (0, h)),
            ],
            scratch_shapes=[pltpu.VMEM((2, q_rows, half), F32)],
        ),
        out_shape=[
            jax.ShapeDtypeStruct((2, q_rows, half), BF16),
            jax.ShapeDtypeStruct((k_rows, heads * DH), BF16),
            jax.ShapeDtypeStruct((k_rows, heads * DH), BF16),
        ],
        compiler_params=pltpu.CompilerParams(vmem_limit_bytes=40 << 20),
        cost_estimate=pl.CostEstimate(
            flops=2 * macs, bytes_accessed=16 << 20, transcendentals=heads * q_rows * k_rows
        ),
    )(scalars, grad, saved_q, saved_k, saved_v, *wo, *wq)


def encoder_kernel(count, quarter, sc, kg_ref, vg_ref, *rest):
    wk, wv, out_ref = rest[:count], rest[count : 2 * count], rest[2 * count]
    per = quarter // BLOCK
    kg, vg = kg_ref[...], vg_ref[...]
    for b in range(count):
        src = sc[b]
        cols = pl.ds(pl.multiple_of((src % per) * BLOCK, BLOCK), BLOCK)
        part = dot(kg, wk[b][...], 1, 0) + dot(vg, wv[b][...], 1, 0)
        out_ref[src // per, :, cols] = part.astype(BF16)


def run_encoder(scalars, kg, vg, wk, wv):
    count = len(wk)
    rows, depth = kg.shape
    quarter = count * BLOCK // 4
    step = 256
    whole = pl.BlockSpec((depth, BLOCK), lambda i, sc: (0, 0))
    return pl.pallas_call(
        functools.partial(encoder_kernel, count, quarter),
        grid_spec=pltpu.PrefetchScalarGridSpec(
            num_scalar_prefetch=1,
            grid=(rows // step,),
            in_specs=[pl.BlockSpec((step, depth), lambda i, sc: (i, 0))] * 2
            + [whole] * (2 * count),
            out_specs=pl.BlockSpec((4, step, quarter), lambda i, sc: (0, i, 0)),
        ),
        out_shape=jax.ShapeDtypeStruct((4, rows, quarter), BF16),
        compiler_params=pltpu.CompilerParams(vmem_limit_bytes=48 << 20),
        cost_estimate=pl.CostEstimate(
            flops=16 * rows * depth * quarter, bytes_accessed=14 << 20, transcendentals=0
        ),
    )(scalars, kg, vg, *wk, *wv)


def pick_kernel(sc, own_ref, other_ref, local_ref, left_ref, right_ref):
    local_ref[...] = (own_ref[...].astype(F32) + other_ref[...].astype(F32)).astype(BF16)
    for c in range(CAP):
        left_ref[c] = local_ref[sc[c]]
        right_ref[c] = local_ref[sc[CAP + c]]


def place_kernel(sc, left_ref, local_ref, right_ref, out_ref):
    tiles = local_ref.shape[0]
    for s in range(tiles):
        i = sc[s]

        @pl.when(i < CAP)
        def _():
            out_ref[s] = left_ref[jnp.minimum(i, CAP - 1)]

        @pl.when((i >= CAP) & (i < CAP + tiles))
        def _():
            out_ref[s] = local_ref[jnp.clip(i - CAP, 0, tiles - 1)]

        @pl.when(i >= CAP + tiles)
        def _():
            out_ref[s] = right_ref[jnp.clip(i - CAP - tiles, 0, CAP - 1)]


def small_call(body, scalars, arrays, outs):
    vmem = pl.BlockSpec(memory_space=pltpu.VMEM)
    single = not isinstance(outs, list)
    return pl.pallas_call(
        body,
        in_specs=[pl.BlockSpec(memory_space=pltpu.SMEM)] + [vmem] * len(arrays),
        out_specs=vmem if single else [vmem] * len(outs),
        out_shape=outs,
        compiler_params=pltpu.CompilerParams(vmem_limit_bytes=24 << 20),
    )(scalars, *arrays)


def gathered(shard):
    full = lax.all_gather(shard, "dp", axis=1, tiled=True)
    blocks = [full[:, i : i + BLOCK] for i in range(0, full.shape[1], BLOCK)]
    return blocks, list(jnp.arange(len(blocks), dtype=jnp.int32))


def fused_kernel(dims, sc, top_ref, q_ref, k_ref, v_ref, wo_ref, wq_ref, wk_ref, wv_ref,
                 sections_ref, parts_ref, wbuf, kg, vg, acc, mixed, other, section, incoming,
                 zs, zr, xs, xr, ms, mr, ss, sr):
    q_rows, k_rows, outer, heads = dims
    half = acc.shape[2]
    per = half // BLOCK
    scale = DH ** (-0.5)
    seg, me, mp = lax.axis_index("segment"), lax.axis_index("dp"), lax.axis_index("mp")
    z, x = me // 2, me % 2
    up = ((z + 1) % outer) * 2 + x
    down = ((z + outer - 1) % outer) * 2 + x
    side = z * 2 + 1 - x
    weights = (wo_ref, wq_ref, wk_ref, wv_ref)
    mesh_id = pl.DeviceIdType.MESH

    barrier = pltpu.get_barrier_semaphore()
    for peer in ((seg, up, mp), (seg, down, mp), (seg, side, mp), (seg, me, 1 - mp), (1 - seg, me, mp)):
        pl.semaphore_signal(barrier, inc=1, device_id=peer, device_id_type=mesh_id)
    pl.semaphore_wait(barrier, 5)

    def block(w, r, sx):
        return weights[w].at[0] if r == 0 and sx == 0 else wbuf.at[w, r * 2 + sx]

    def source(r, sx):
        return ((z + outer - r) % outer) * 2 + (x if sx == 0 else 1 - x)

    def send(src, dst, a, b, peer):
        return pltpu.make_async_remote_copy(
            src_ref=src, dst_ref=dst, send_sem=a, recv_sem=b, device_id=peer, device_id_type=mesh_id
        )

    def z_copy(w, r):
        return send(block(w, r, 0), block(w, r + 1, 0), zs.at[w, r], zr.at[w, r], (seg, up, mp))

    def x_copy(w, r):
        return send(block(w, r, 0), block(w, r, 1), xs.at[w, r], xr.at[w, r], (seg, side, mp))

    def advance(pair, r):
        for w in pair:
            if r > 0:
                z_copy(w, r - 1).wait_recv()
            if r < outer - 1:
                z_copy(w, r).start()
            x_copy(w, r).start()

    def arrive(pair):
        for w in pair:
            for r in range(outer):
                x_copy(w, r).wait_recv()

    slots = [(r, sx) for r in range(outer) for sx in range(2)]

    def tick(s, grad):
        acc[...] = jnp.zeros_like(acc)

        def one_head(h, carry):
            hs = pl.ds(pl.multiple_of(h * DH, DH), DH)
            og = jnp.zeros((q_rows, DH), F32)
            for r, sx in slots:
                og += dot(grad(source(r, sx)), block(0, r, sx)[hs, :], 1, 1)
            og = og.astype(BF16)
            q = q_ref[0, s * q_rows : (s + 1) * q_rows, hs]
            k = k_ref[0, s * k_rows : (s + 1) * k_rows, hs]
            v = v_ref[0, s * k_rows : (s + 1) * k_rows, hs]
            scores = dot(q, k, 1, 1) * scale
            rows = lax.broadcasted_iota(jnp.int32, scores.shape, 0)
            cols = lax.broadcasted_iota(jnp.int32, scores.shape, 1)
            allowed = None
            for e in range(2):
                q_len, k_off, k_len = sc[s, e], sc[s, 2 + e] * TILE, sc[s, 4 + e]
                hit = (rows >= e * TILE) & (rows < e * TILE + q_len)
                hit = hit & (cols >= k_off) & (cols < k_off + k_len)
                allowed = hit if allowed is None else allowed | hit
            masked = jnp.where(allowed, scores, masked_floor)
            peak = jnp.max(masked, axis=-1, keepdims=True)
            terms = jnp.where(allowed, jnp.exp(masked - peak), 0.0)
            prob = terms / jnp.maximum(jnp.sum(terms, axis=-1, keepdims=True), 1.0)
            prob_bf = prob.astype(BF16)
            attended = dot(prob_bf, v, 1, 0)
            out_dot = jnp.sum(og.astype(F32) * attended, axis=-1, keepdims=True)
            sg = (prob * (dot(og, v, 1, 1) - out_dot)).astype(BF16)
            qg = (dot(sg, k, 1, 0) * scale).astype(BF16)
            kg[s * k_rows : (s + 1) * k_rows, hs] = (dot(sg, q, 0, 0) * scale).astype(BF16)
            vg[s * k_rows : (s + 1) * k_rows, hs] = dot(prob_bf, og, 0, 0).astype(BF16)
            for r, sx in slots:
                src = source(r, sx)
                at = pl.ds(pl.multiple_of((src % per) * BLOCK, BLOCK), BLOCK)
                acc[src // per, :, at] += dot(qg, block(1, r, sx)[hs, :], 1, 0)
            return carry

        lax.fori_loop(0, heads, one_head, 0)
        mixed[s] = acc[...].astype(BF16)

    def top_block(s):
        def load(src):
            at = pl.ds(pl.multiple_of(src * BLOCK, BLOCK), BLOCK)
            return top_ref[s * q_rows : (s + 1) * q_rows, at]

        return load

    def incoming_block(s):
        def load(src):
            at = pl.ds(pl.multiple_of((src % per) * BLOCK, BLOCK), BLOCK)
            return incoming[s, src // per, :, at]

        return load

    def upper_copy(s):
        return send(mixed.at[s], other.at[s], ms.at[0, s], mr.at[0, s], (seg, me, 1 - mp))

    def lower_copy(s):
        return send(mixed.at[s, 1 - mp], other.at[s, 0], ms.at[1, s], mr.at[1, s], (seg, me, 1 - mp))

    def layer_copy(s):
        return send(section.at[s], incoming.at[s], ss.at[s], sr.at[s], (1 - seg, me, mp))

    def finish_upper(s):
        upper_copy(s).wait_recv()
        rows = slice(s * q_rows, (s + 1) * q_rows)
        for i in range(2):
            base = top_ref[rows, i * half : (i + 1) * half].astype(F32)
            total = base + (mixed[s, i].astype(F32) + other[s, i].astype(F32))
            section[s, i] = total.astype(BF16)
        layer_copy(s).start()
        sections_ref[0, rows, :] = section[s, mp]

    def finish_lower(s):
        lower_copy(s).wait_recv()
        rows = slice(s * q_rows, (s + 1) * q_rows)
        total = mixed[s, mp].astype(F32) + other[s, 0].astype(F32)
        sections_ref[0, rows, :] = (incoming[s, mp].astype(F32) + total).astype(BF16)

    for r in range(outer):
        advance((0, 1), r)
    advance((2, 3), 0)
    arrive((0, 1))

    @pl.when(seg == 1)
    def _():
        tick(0, top_block(0))
        upper_copy(0).start()

    advance((2, 3), 1)

    @pl.when(seg == 1)
    def _():
        tick(1, top_block(1))
        upper_copy(1).start()
        finish_upper(0)

    for r in range(2, outer - 1):
        advance((2, 3), r)

    @pl.when(seg == 1)
    def _():
        finish_upper(1)

    @pl.when(seg == 0)
    def _():
        layer_copy(0).wait_recv()
        tick(0, incoming_block(0))
        lower_copy(0).start()

    advance((2, 3), outer - 1)

    @pl.when(seg == 0)
    def _():
        layer_copy(1).wait_recv()
        tick(1, incoming_block(1))
        lower_copy(1).start()
        finish_lower(0)

    arrive((2, 3))
    quarter = parts_ref.shape[2]
    step = 256

    def encode(i, carry):
        rows = pl.ds(pl.multiple_of(i * step, step), step)
        for r, sx in slots:
            src = source(r, sx)
            each = quarter // BLOCK
            at = pl.ds(pl.multiple_of((src % each) * BLOCK, BLOCK), BLOCK)
            part = dot(kg[rows, :], block(2, r, sx)[...], 1, 0)
            part += dot(vg[rows, :], block(3, r, sx)[...], 1, 0)
            parts_ref[src // each, rows, at] = part.astype(BF16)
        return carry

    lax.fori_loop(0, kg.shape[0] // step, encode, 0)

    @pl.when(seg == 0)
    def _():
        finish_lower(1)
        for s in range(2):
            lower_copy(s).wait_send()

    @pl.when(seg == 1)
    def _():
        for s in range(2):
            upper_copy(s).wait_send()
            layer_copy(s).wait_send()

    for w in range(4):
        for r in range(outer):
            x_copy(w, r).wait_send()
            if r < outer - 1:
                z_copy(w, r).wait_send()


def run_fused(scalars, top, q, k, v, wo, wq, wk, wv, outer):
    micro = scalars.shape[0]
    q_rows, k_rows = top.shape[0] // micro, k.shape[1] // micro
    width, depth = top.shape[1], q.shape[2]
    half = width // 2
    vmem = pl.BlockSpec(memory_space=pltpu.VMEM)
    dma = pltpu.SemaphoreType.DMA
    return pl.pallas_call(
        functools.partial(fused_kernel, (q_rows, k_rows, outer, depth // DH)),
        in_specs=[pl.BlockSpec(memory_space=pltpu.SMEM)] + [vmem] * 8,
        out_specs=[vmem, vmem],
        out_shape=[
            jax.ShapeDtypeStruct((1, micro * q_rows, half), BF16),
            jax.ShapeDtypeStruct((4, micro * k_rows, width // 4), BF16),
        ],
        scratch_shapes=[
            pltpu.VMEM((4, 2 * outer, depth, BLOCK), BF16),
            pltpu.VMEM((micro * k_rows, depth), BF16),
            pltpu.VMEM((micro * k_rows, depth), BF16),
            pltpu.VMEM((2, q_rows, half), F32),
        ]
        + [pltpu.VMEM((micro, 2, q_rows, half), BF16)] * 4
        + [dma((4, outer))] * 4
        + [dma((2, micro))] * 2
        + [dma((micro,))] * 2,
        compiler_params=pltpu.CompilerParams(
            collective_id=0, has_side_effects=True, vmem_limit_bytes=58 << 20
        ),
    )(scalars, top, q, k, v, wo, wq, wk, wv)


def ranked(marked):
    ids = jnp.arange(marked.shape[0], dtype=jnp.int32)
    upto = ids[None, :] <= ids[:, None]
    return jnp.sum((upto & marked[None, :]).astype(jnp.int32), axis=1) - 1


def on_device(
    grad_top,
    saved_query,
    saved_key,
    saved_value,
    w_query,
    w_key,
    w_value,
    w_out,
    query_length,
    key_offset,
    key_length,
    tile_owner,
):
    seg = lax.axis_index("segment")
    mp = lax.axis_index("mp")
    devices = lax.axis_size("dp")
    me = lax.axis_index("dp")
    micro = query_length.shape[0]
    q_rows = grad_top.shape[0] // micro
    k_rows = saved_key.shape[1] // micro
    half = grad_top.shape[1] // 2
    mp_swap = [(0, 1), (1, 0)]
    if w_out.shape[2] == BLOCK and devices % 2 == 0 and devices > 4 and micro == 2:
        table = jnp.concatenate([query_length, key_offset, key_length], axis=1)
        sections, parts = run_fused(
            table, grad_top, saved_query, saved_key, saved_value, w_out, w_query, w_key, w_value,
            devices // 2,
        )
    else:
        wo, sources = gathered(w_out[0])
        wq, _ = gathered(w_query[0])
        wk, _ = gathered(w_key[0])
        wv, _ = gathered(w_value[0])
        order = jnp.stack(sources).astype(jnp.int32)

        top = grad_top.reshape(grad_top.shape[0], 2, half).transpose(1, 0, 2)
        scalars = [
            jnp.concatenate([order, query_length[s], key_offset[s], key_length[s]])
            for s in range(micro)
        ]

        def tick(s, grad, at):
            return run_tick(
                scalars[s], grad, at, s, saved_query, saved_key, saved_value, wo, wq, q_rows, k_rows
            )

        upper = [tick(s, top, s) for s in range(micro)]
        upper_half, incoming = [], []
        for s in range(micro):
            mixed = upper[s][0]
            other = lax.ppermute(mixed, "mp", mp_swap)
            rows = top[:, s * q_rows : (s + 1) * q_rows]
            section = (rows.astype(F32) + (mixed.astype(F32) + other.astype(F32))).astype(BF16)
            incoming.append(lax.ppermute(section, "segment", [(1, 0)]))
            upper_half.append(lax.dynamic_index_in_dim(section, mp, 0, keepdims=False))
        lower = [tick(s, incoming[s], 0) for s in range(micro)]
        halves = []
        for s in range(micro):
            mixed = lower[s][0]
            other = lax.ppermute(
                lax.dynamic_index_in_dim(mixed, 1 - mp, 0, keepdims=False), "mp", mp_swap
            )
            own = lax.dynamic_index_in_dim(mixed, mp, 0, keepdims=False)
            base = lax.dynamic_index_in_dim(incoming[s], mp, 0, keepdims=False)
            low = (base.astype(F32) + (own.astype(F32) + other.astype(F32))).astype(BF16)
            halves.append(jnp.where(seg == 1, upper_half[s], low))
        sections = jnp.concatenate(halves, axis=0)[None]

        kg = jnp.concatenate([jnp.where(seg == 1, upper[s][1], lower[s][1]) for s in range(micro)], 0)
        vg = jnp.concatenate([jnp.where(seg == 1, upper[s][2], lower[s][2]) for s in range(micro)], 0)
        parts = run_encoder(order, kg, vg, wk, wv)
    away = lax.dynamic_slice_in_dim(parts, (1 - seg) * 2, 2, 0)
    mine = lax.dynamic_slice_in_dim(parts, seg * 2, 2, 0)
    arrived = lax.ppermute(away, "segment", mp_swap)
    summed = (mine.astype(F32) + arrived.astype(F32)).astype(BF16)
    crossing = lax.ppermute(
        lax.dynamic_index_in_dim(summed, 1 - mp, 0, keepdims=False), "mp", mp_swap
    )
    kept = lax.dynamic_index_in_dim(summed, mp, 0, keepdims=False)

    tiles = kept.shape[0] // TILE
    features = kept.shape[1]
    owners = tile_owner.reshape(devices, tiles)
    slot_ids = jnp.arange(CAP, dtype=jnp.int32)[:, None]
    tile_ids = jnp.arange(tiles, dtype=jnp.int32)

    def plan(source):
        source = source % devices
        row = lax.dynamic_index_in_dim(owners, source, 0, keepdims=False)
        return (row // tiles - source + devices) % devices, row % tiles

    def ranks_of(marked):
        return (ranked(marked)[None, :] == slot_ids) & marked[None, :]

    step, slot = plan(me)
    left_step, left_slot = plan(me - 1 + devices)
    right_step, right_slot = plan(me + 1)
    send_left = jnp.sum(jnp.where(ranks_of(step == devices - 1), tile_ids[None, :], 0), axis=1)
    send_right = jnp.sum(jnp.where(ranks_of(step == 1), tile_ids[None, :], 0), axis=1)
    left_hit = ranks_of(left_step == 1)
    right_hit = ranks_of(right_step == devices - 1)
    target = jnp.concatenate(
        [
            jnp.sum(jnp.where(left_hit, left_slot[None, :], 0), axis=1),
            slot,
            jnp.sum(jnp.where(right_hit, right_slot[None, :], 0), axis=1),
        ]
    )
    usable = jnp.concatenate([jnp.any(left_hit, axis=1), step == 0, jnp.any(right_hit, axis=1)])
    chosen = (tile_ids[:, None] == target[None, :]) & usable[None, :]
    candidate_ids = jnp.arange(target.shape[0], dtype=jnp.int32)
    take = jnp.sum(jnp.where(chosen, candidate_ids[None, :], 0), axis=1)

    tiled = (tiles, TILE, features)
    shape = jax.ShapeDtypeStruct(tiled, BF16)
    handed = jax.ShapeDtypeStruct((CAP, TILE, features), BF16)
    local, to_left, to_right = small_call(
        pick_kernel,
        jnp.concatenate([send_left, send_right]),
        [kept.reshape(tiled), crossing.reshape(tiled)],
        [shape, handed, handed],
    )
    forward = [(i, (i + 1) % devices) for i in range(devices)]
    backward = [(b, a) for a, b in forward]
    from_left = lax.ppermute(to_right, "dp", forward)
    from_right = lax.ppermute(to_left, "dp", backward)
    owned = small_call(place_kernel, take, [from_left, local, from_right], shape)
    return sections, owned.reshape(tiles * TILE, features)


def solution(mesh):
    in_specs = (
        P("dp", None),
        P("segment", "dp", "mp"),
        P("segment", "dp", "mp"),
        P("segment", "dp", "mp"),
        P("segment", "mp", "dp"),
        P("segment", "mp", "dp"),
        P("segment", "mp", "dp"),
        P("segment", "mp", "dp"),
        P("dp", None),
        P("dp", None),
        P("dp", None),
        P(),
    )
    out_specs = (P("segment", "dp", "mp"), P("dp", ("segment", "mp")))
    return jax.shard_map(
        on_device, mesh=mesh, in_specs=in_specs, out_specs=out_specs, check_vma=False
    )
```

```python
import functools

import jax
import jax.numpy as jnp
from jax import lax
from jax.experimental import pallas as pl
from jax.experimental.pallas import tpu as pltpu
from jax.sharding import PartitionSpec as P

DH = 256
TILE = 128
CAP = 2
BLOCK = 256
masked_floor = -1e30
BF16, F32 = jnp.bfloat16, jnp.float32


def dot(a, b, ca, cb):
    return lax.dot_general(a, b, (((ca,), (cb,)), ((), ())), preferred_element_type=F32)


def tick_kernel(count, half, sc, g_ref, q_ref, k_ref, v_ref, *rest):
    wo, wq = rest[:count], rest[count : 2 * count]
    mixed_ref, kg_ref, vg_ref, acc = rest[2 * count :]
    head = pl.program_id(0)
    per = half // BLOCK
    scale = DH ** (-0.5)

    def place(b):
        src = sc[b]
        return src // per, pl.ds(pl.multiple_of((src % per) * BLOCK, BLOCK), BLOCK)

    og = None
    for b in range(count):
        at, cols = place(b)
        term = dot(g_ref[at, :, cols], wo[b][...], 1, 1)
        og = term if og is None else og + term
    og = og.astype(BF16)
    q, k, v = q_ref[0], k_ref[0], v_ref[0]
    scores = dot(q, k, 1, 1) * scale
    rows = lax.broadcasted_iota(jnp.int32, scores.shape, 0)
    cols_id = lax.broadcasted_iota(jnp.int32, scores.shape, 1)
    allowed = None
    for e in range(2):
        q_len, k_off, k_len = sc[count + e], sc[count + 2 + e] * TILE, sc[count + 4 + e]
        hit = (rows >= e * TILE) & (rows < e * TILE + q_len)
        hit = hit & (cols_id >= k_off) & (cols_id < k_off + k_len)
        allowed = hit if allowed is None else allowed | hit
    masked = jnp.where(allowed, scores, masked_floor)
    top = jnp.max(masked, axis=-1, keepdims=True)
    terms = jnp.where(allowed, jnp.exp(masked - top), 0.0)
    prob = terms / jnp.maximum(jnp.sum(terms, axis=-1, keepdims=True), 1.0)
    prob_bf = prob.astype(BF16)
    attended = dot(prob_bf, v, 1, 0)
    out_dot = jnp.sum(og.astype(F32) * attended, axis=-1, keepdims=True)
    sg = (prob * (dot(og, v, 1, 1) - out_dot)).astype(BF16)
    qg = (dot(sg, k, 1, 0) * scale).astype(BF16)
    kg_ref[...] = (dot(sg, q, 0, 0) * scale).astype(BF16)
    vg_ref[...] = dot(prob_bf, og, 0, 0).astype(BF16)

    @pl.when(head == 0)
    def _():
        acc[...] = jnp.zeros_like(acc)

    for b in range(count):
        at, cols = place(b)
        acc[at, :, cols] += dot(qg, wq[b][...], 1, 0)

    @pl.when(head == pl.num_programs(0) - 1)
    def _():
        mixed_ref[...] = acc[...].astype(BF16)


def run_tick(scalars, grad, at, seq, saved_q, saved_k, saved_v, wo, wq, q_rows, k_rows):
    half = grad.shape[2]
    heads = saved_q.shape[2] // DH
    count = len(wo)
    weight = pl.BlockSpec((DH, BLOCK), lambda h, sc: (h, 0))
    macs = heads * q_rows * DH * (4 * half + 6 * k_rows)
    return pl.pallas_call(
        functools.partial(tick_kernel, count, half),
        grid_spec=pltpu.PrefetchScalarGridSpec(
            num_scalar_prefetch=1,
            grid=(heads,),
            in_specs=[
                pl.BlockSpec((2, q_rows, half), lambda h, sc: (0, at, 0)),
                pl.BlockSpec((1, q_rows, DH), lambda h, sc: (0, seq, h)),
                pl.BlockSpec((1, k_rows, DH), lambda h, sc: (0, seq, h)),
                pl.BlockSpec((1, k_rows, DH), lambda h, sc: (0, seq, h)),
            ]
            + [weight] * (2 * count),
            out_specs=[
                pl.BlockSpec((2, q_rows, half), lambda h, sc: (0, 0, 0)),
                pl.BlockSpec((k_rows, DH), lambda h, sc: (0, h)),
                pl.BlockSpec((k_rows, DH), lambda h, sc: (0, h)),
            ],
            scratch_shapes=[pltpu.VMEM((2, q_rows, half), F32)],
        ),
        out_shape=[
            jax.ShapeDtypeStruct((2, q_rows, half), BF16),
            jax.ShapeDtypeStruct((k_rows, heads * DH), BF16),
            jax.ShapeDtypeStruct((k_rows, heads * DH), BF16),
        ],
        compiler_params=pltpu.CompilerParams(vmem_limit_bytes=40 << 20),
        cost_estimate=pl.CostEstimate(
            flops=2 * macs, bytes_accessed=16 << 20, transcendentals=heads * q_rows * k_rows
        ),
    )(scalars, grad, saved_q, saved_k, saved_v, *wo, *wq)


def encoder_kernel(count, quarter, sc, kg_ref, vg_ref, *rest):
    wk, wv, out_ref = rest[:count], rest[count : 2 * count], rest[2 * count]
    per = quarter // BLOCK
    kg, vg = kg_ref[...], vg_ref[...]
    for b in range(count):
        src = sc[b]
        cols = pl.ds(pl.multiple_of((src % per) * BLOCK, BLOCK), BLOCK)
        part = dot(kg, wk[b][...], 1, 0) + dot(vg, wv[b][...], 1, 0)
        out_ref[src // per, :, cols] = part.astype(BF16)


def run_encoder(scalars, kg, vg, wk, wv):
    count = len(wk)
    rows, depth = kg.shape
    quarter = count * BLOCK // 4
    step = 256
    whole = pl.BlockSpec((depth, BLOCK), lambda i, sc: (0, 0))
    return pl.pallas_call(
        functools.partial(encoder_kernel, count, quarter),
        grid_spec=pltpu.PrefetchScalarGridSpec(
            num_scalar_prefetch=1,
            grid=(rows // step,),
            in_specs=[pl.BlockSpec((step, depth), lambda i, sc: (i, 0))] * 2
            + [whole] * (2 * count),
            out_specs=pl.BlockSpec((4, step, quarter), lambda i, sc: (0, i, 0)),
        ),
        out_shape=jax.ShapeDtypeStruct((4, rows, quarter), BF16),
        compiler_params=pltpu.CompilerParams(vmem_limit_bytes=48 << 20),
        cost_estimate=pl.CostEstimate(
            flops=16 * rows * depth * quarter, bytes_accessed=14 << 20, transcendentals=0
        ),
    )(scalars, kg, vg, *wk, *wv)


def pick_kernel(sc, local_ref, left_ref, right_ref):
    for c in range(CAP):
        left_ref[c] = local_ref[sc[c]]
        right_ref[c] = local_ref[sc[CAP + c]]


def place_kernel(sc, left_ref, local_ref, right_ref, out_ref):
    tiles = local_ref.shape[0]
    for s in range(tiles):
        i = sc[s]

        @pl.when(i < CAP)
        def _():
            out_ref[s] = left_ref[jnp.minimum(i, CAP - 1)]

        @pl.when((i >= CAP) & (i < CAP + tiles))
        def _():
            out_ref[s] = local_ref[jnp.clip(i - CAP, 0, tiles - 1)]

        @pl.when(i >= CAP + tiles)
        def _():
            out_ref[s] = right_ref[jnp.clip(i - CAP - tiles, 0, CAP - 1)]


def small_call(body, scalars, arrays, outs):
    vmem = pl.BlockSpec(memory_space=pltpu.VMEM)
    single = not isinstance(outs, list)
    return pl.pallas_call(
        body,
        in_specs=[pl.BlockSpec(memory_space=pltpu.SMEM)] + [vmem] * len(arrays),
        out_specs=vmem if single else [vmem] * len(outs),
        out_shape=outs,
        compiler_params=pltpu.CompilerParams(vmem_limit_bytes=24 << 20),
    )(scalars, *arrays)


def gathered(shard):
    full = lax.all_gather(shard, "dp", axis=1, tiled=True)
    blocks = [full[:, i : i + BLOCK] for i in range(0, full.shape[1], BLOCK)]
    return blocks, list(jnp.arange(len(blocks), dtype=jnp.int32))


def fused_kernel(dims, sc, top_ref, q_ref, k_ref, v_ref, wo_ref, wq_ref, wk_ref, wv_ref,
                 sections_ref, local_ref, wbuf, kg, vg, acc, mixed, other, section, incoming,
                 parts, arrived, summed, crossed,
                 zs, zr, xs, xr, ms, mr, ss, sr, es, er, ps, pr, ys, yr):
    q_rows, k_rows, outer, heads = dims
    half = acc.shape[2]
    per = half // BLOCK
    scale = DH ** (-0.5)
    seg, me, mp = lax.axis_index("segment"), lax.axis_index("dp"), lax.axis_index("mp")
    z, x = me // 2, me % 2
    up = ((z + 1) % outer) * 2 + x
    down = ((z + outer - 1) % outer) * 2 + x
    side = z * 2 + 1 - x
    weights = (wo_ref, wq_ref, wk_ref, wv_ref)
    mesh_id = pl.DeviceIdType.MESH

    barrier = pltpu.get_barrier_semaphore()
    for peer in ((seg, up, mp), (seg, down, mp), (seg, side, mp), (seg, me, 1 - mp), (1 - seg, me, mp)):
        pl.semaphore_signal(barrier, inc=1, device_id=peer, device_id_type=mesh_id)
    pl.semaphore_wait(barrier, 5)

    def block(w, r, sx):
        return weights[w].at[0] if r == 0 and sx == 0 else wbuf.at[w, r * 2 + sx]

    def source(r, sx):
        return ((z + outer - r) % outer) * 2 + (x if sx == 0 else 1 - x)

    def send(src, dst, a, b, peer):
        return pltpu.make_async_remote_copy(
            src_ref=src, dst_ref=dst, send_sem=a, recv_sem=b, device_id=peer, device_id_type=mesh_id
        )

    def z_copy(w, r):
        return send(block(w, r, 0), block(w, r + 1, 0), zs.at[w, r], zr.at[w, r], (seg, up, mp))

    last = outer - 1
    depth = kg.shape[1]
    upper_rows, lower_rows = pl.ds(0, depth // 2), pl.ds(depth // 2, depth // 2)

    def x_copy(w, r):
        src, dst = block(w, r, 0), block(w, r, 1)
        if r == last:
            src, dst = src.at[upper_rows], dst.at[upper_rows]
        return send(src, dst, xs.at[w, r], xr.at[w, r], (seg, side, mp))

    def extra_copy(w):
        src, dst = block(w, last - 1, 1).at[lower_rows], block(w, last, 1).at[lower_rows]
        return send(src, dst, es.at[w], er.at[w], (seg, up, mp))

    def extras(pair):
        for w in pair:
            x_copy(w, last - 1).wait_recv()
            extra_copy(w).start()

    def advance(pair, r):
        for w in pair:
            if r > 0:
                z_copy(w, r - 1).wait_recv()
            if r < outer - 1:
                z_copy(w, r).start()
            x_copy(w, r).start()

    def arrive(pair, r):
        for w in pair:
            if r != last - 1:
                x_copy(w, r).wait_recv()
            if r == last:
                extra_copy(w).wait_recv()

    slots = [(r, sx) for r in range(outer) for sx in range(2)]

    def tick(s, grad):
        acc[...] = jnp.zeros_like(acc)

        def one_head(h, carry):
            hs = pl.ds(pl.multiple_of(h * DH, DH), DH)
            og = jnp.zeros((q_rows, DH), F32)
            for r, sx in slots:
                og += dot(grad(source(r, sx)), block(0, r, sx)[hs, :], 1, 1)
            og = og.astype(BF16)
            q = q_ref[0, s * q_rows : (s + 1) * q_rows, hs]
            k = k_ref[0, s * k_rows : (s + 1) * k_rows, hs]
            v = v_ref[0, s * k_rows : (s + 1) * k_rows, hs]
            scores = dot(q, k, 1, 1) * scale
            rows = lax.broadcasted_iota(jnp.int32, scores.shape, 0)
            cols = lax.broadcasted_iota(jnp.int32, scores.shape, 1)
            allowed = None
            for e in range(2):
                q_len, k_off, k_len = sc[s, e], sc[s, 2 + e] * TILE, sc[s, 4 + e]
                hit = (rows >= e * TILE) & (rows < e * TILE + q_len)
                hit = hit & (cols >= k_off) & (cols < k_off + k_len)
                allowed = hit if allowed is None else allowed | hit
            masked = jnp.where(allowed, scores, masked_floor)
            peak = jnp.max(masked, axis=-1, keepdims=True)
            terms = jnp.where(allowed, jnp.exp(masked - peak), 0.0)
            prob = terms / jnp.maximum(jnp.sum(terms, axis=-1, keepdims=True), 1.0)
            prob_bf = prob.astype(BF16)
            attended = dot(prob_bf, v, 1, 0)
            out_dot = jnp.sum(og.astype(F32) * attended, axis=-1, keepdims=True)
            sg = (prob * (dot(og, v, 1, 1) - out_dot)).astype(BF16)
            qg = (dot(sg, k, 1, 0) * scale).astype(BF16)
            kg[s * k_rows : (s + 1) * k_rows, hs] = (dot(sg, q, 0, 0) * scale).astype(BF16)
            vg[s * k_rows : (s + 1) * k_rows, hs] = dot(prob_bf, og, 0, 0).astype(BF16)
            for r, sx in slots:
                src = source(r, sx)
                at = pl.ds(pl.multiple_of((src % per) * BLOCK, BLOCK), BLOCK)
                acc[src // per, :, at] += dot(qg, block(1, r, sx)[hs, :], 1, 0)
            return carry

        lax.fori_loop(0, heads, one_head, 0)
        mixed[s] = acc[...].astype(BF16)

    def top_block(s):
        def load(src):
            at = pl.ds(pl.multiple_of(src * BLOCK, BLOCK), BLOCK)
            return top_ref[s * q_rows : (s + 1) * q_rows, at]

        return load

    def incoming_block(s):
        def load(src):
            at = pl.ds(pl.multiple_of((src % per) * BLOCK, BLOCK), BLOCK)
            return incoming[s, src // per, :, at]

        return load

    def upper_copy(s):
        return send(mixed.at[s], other.at[s], ms.at[0, s], mr.at[0, s], (seg, me, 1 - mp))

    def lower_copy(s):
        return send(mixed.at[s, 1 - mp], other.at[s, 0], ms.at[1, s], mr.at[1, s], (seg, me, 1 - mp))

    def layer_copy(s):
        return send(section.at[s], incoming.at[s], ss.at[s], sr.at[s], (1 - seg, me, mp))

    def finish_upper(s):
        upper_copy(s).wait_recv()
        rows = slice(s * q_rows, (s + 1) * q_rows)
        for i in range(2):
            base = top_ref[rows, i * half : (i + 1) * half].astype(F32)
            total = base + (mixed[s, i].astype(F32) + other[s, i].astype(F32))
            section[s, i] = total.astype(BF16)
        layer_copy(s).start()
        sections_ref[0, rows, :] = section[s, mp]

    def finish_lower(s):
        lower_copy(s).wait_recv()
        rows = slice(s * q_rows, (s + 1) * q_rows)
        total = mixed[s, mp].astype(F32) + other[s, 0].astype(F32)
        sections_ref[0, rows, :] = (incoming[s, mp].astype(F32) + total).astype(BF16)

    for r in range(outer):
        advance((0, 1), r)
    extras((0, 1))
    advance((2, 3), 0)
    for r in range(outer):
        arrive((0, 1), r)

    @pl.when(seg == 1)
    def _():
        tick(0, top_block(0))
        upper_copy(0).start()

    advance((2, 3), 1)

    @pl.when(seg == 1)
    def _():
        tick(1, top_block(1))
        upper_copy(1).start()
        finish_upper(0)

    for r in range(2, outer - 1):
        advance((2, 3), r)

    @pl.when(seg == 1)
    def _():
        finish_upper(1)

    @pl.when(seg == 0)
    def _():
        layer_copy(0).wait_recv()
        tick(0, incoming_block(0))
        lower_copy(0).start()

    advance((2, 3), last)
    extras((2, 3))

    @pl.when(seg == 0)
    def _():
        layer_copy(1).wait_recv()
        tick(1, incoming_block(1))
        lower_copy(1).start()
        finish_lower(0)

    step = 256

    def quarter_of(r):
        return (z + outer - r) % outer

    def part_copy(r):
        q = quarter_of(r)
        return send(parts.at[q], arrived.at[q % 2], ps.at[r], pr.at[r], (1 - seg, me, mp))

    def cross_copy(r):
        return send(summed.at[quarter_of(r) % 2], crossed, ys.at[0], yr.at[0], (seg, me, 1 - mp))

    def encode(r):
        q = quarter_of(r)

        def rows_step(i, carry):
            rows = pl.ds(pl.multiple_of(i * step, step), step)
            for sx in range(2):
                at = pl.ds(pl.multiple_of((x if sx == 0 else 1 - x) * BLOCK, BLOCK), BLOCK)
                part = dot(kg[rows, :], block(2, r, sx)[...], 1, 0)
                part += dot(vg[rows, :], block(3, r, sx)[...], 1, 0)
                parts[q, rows, at] = part.astype(BF16)
            return carry

        lax.fori_loop(0, kg.shape[0] // step, rows_step, 0)

        @pl.when(seg != q // 2)
        def _():
            part_copy(r).start()

    def reduce(r):
        q = quarter_of(r)

        @pl.when(seg == q // 2)
        def _():
            part_copy(r).wait_recv()
            summed[q % 2] = (parts[q].astype(F32) + arrived[q % 2].astype(F32)).astype(BF16)

            @pl.when(mp != q % 2)
            def _():
                cross_copy(r).start()

    for r in range(outer):
        if r == last:

            @pl.when(seg == 0)
            def _():
                finish_lower(1)

        arrive((2, 3), r)
        encode(r)
        if r > 0:
            reduce(r - 1)
    reduce(last)
    cross_copy(0).wait_recv()
    local_ref[...] = (summed[mp].astype(F32) + crossed[...].astype(F32)).astype(BF16)
    cross_copy(0).wait_send()
    for r in range(outer):

        @pl.when(seg != quarter_of(r) // 2)
        def _():
            part_copy(r).wait_send()

    @pl.when(seg == 0)
    def _():
        for s in range(2):
            lower_copy(s).wait_send()

    @pl.when(seg == 1)
    def _():
        for s in range(2):
            upper_copy(s).wait_send()
            layer_copy(s).wait_send()

    for w in range(4):
        for r in range(outer):
            x_copy(w, r).wait_send()
            if r == last:
                extra_copy(w).wait_send()
            if r < outer - 1:
                z_copy(w, r).wait_send()


def run_fused(scalars, top, q, k, v, wo, wq, wk, wv, outer):
    micro = scalars.shape[0]
    q_rows, k_rows = top.shape[0] // micro, k.shape[1] // micro
    width, depth = top.shape[1], q.shape[2]
    half = width // 2
    vmem = pl.BlockSpec(memory_space=pltpu.VMEM)
    dma = pltpu.SemaphoreType.DMA
    return pl.pallas_call(
        functools.partial(fused_kernel, (q_rows, k_rows, outer, depth // DH)),
        in_specs=[pl.BlockSpec(memory_space=pltpu.SMEM)] + [vmem] * 8,
        out_specs=[vmem, vmem],
        out_shape=[
            jax.ShapeDtypeStruct((1, micro * q_rows, half), BF16),
            jax.ShapeDtypeStruct((micro * k_rows, width // 4), BF16),
        ],
        scratch_shapes=[
            pltpu.VMEM((4, 2 * outer, depth, BLOCK), BF16),
            pltpu.VMEM((micro * k_rows, depth), BF16),
            pltpu.VMEM((micro * k_rows, depth), BF16),
            pltpu.VMEM((2, q_rows, half), F32),
        ]
        + [pltpu.VMEM((micro, 2, q_rows, half), BF16)] * 4
        + [pltpu.VMEM((n, micro * k_rows, width // 4), BF16) for n in (4, 2, 2)]
        + [pltpu.VMEM((micro * k_rows, width // 4), BF16)]
        + [dma((4, outer))] * 4
        + [dma((2, micro))] * 2
        + [dma((micro,))] * 2
        + [dma((4,))] * 2
        + [dma((outer,))] * 2
        + [dma((1,))] * 2,
        compiler_params=pltpu.CompilerParams(
            collective_id=0, has_side_effects=True, vmem_limit_bytes=58 << 20
        ),
    )(scalars, top, q, k, v, wo, wq, wk, wv)


def ranked(marked):
    ids = jnp.arange(marked.shape[0], dtype=jnp.int32)
    upto = ids[None, :] <= ids[:, None]
    return jnp.sum((upto & marked[None, :]).astype(jnp.int32), axis=1) - 1


def on_device(
    grad_top,
    saved_query,
    saved_key,
    saved_value,
    w_query,
    w_key,
    w_value,
    w_out,
    query_length,
    key_offset,
    key_length,
    tile_owner,
):
    seg = lax.axis_index("segment")
    mp = lax.axis_index("mp")
    devices = lax.axis_size("dp")
    me = lax.axis_index("dp")
    micro = query_length.shape[0]
    q_rows = grad_top.shape[0] // micro
    k_rows = saved_key.shape[1] // micro
    half = grad_top.shape[1] // 2
    mp_swap = [(0, 1), (1, 0)]
    if w_out.shape[2] == BLOCK and devices == 8 and micro == 2:
        table = jnp.concatenate([query_length, key_offset, key_length], axis=1)
        sections, kept = run_fused(
            table, grad_top, saved_query, saved_key, saved_value, w_out, w_query, w_key, w_value,
            devices // 2,
        )
    else:
        wo, sources = gathered(w_out[0])
        wq, _ = gathered(w_query[0])
        wk, _ = gathered(w_key[0])
        wv, _ = gathered(w_value[0])
        order = jnp.stack(sources).astype(jnp.int32)

        top = grad_top.reshape(grad_top.shape[0], 2, half).transpose(1, 0, 2)
        scalars = [
            jnp.concatenate([order, query_length[s], key_offset[s], key_length[s]])
            for s in range(micro)
        ]

        def tick(s, grad, at):
            return run_tick(
                scalars[s], grad, at, s, saved_query, saved_key, saved_value, wo, wq, q_rows, k_rows
            )

        upper = [tick(s, top, s) for s in range(micro)]
        upper_half, incoming = [], []
        for s in range(micro):
            mixed = upper[s][0]
            other = lax.ppermute(mixed, "mp", mp_swap)
            rows = top[:, s * q_rows : (s + 1) * q_rows]
            section = (rows.astype(F32) + (mixed.astype(F32) + other.astype(F32))).astype(BF16)
            incoming.append(lax.ppermute(section, "segment", [(1, 0)]))
            upper_half.append(lax.dynamic_index_in_dim(section, mp, 0, keepdims=False))
        lower = [tick(s, incoming[s], 0) for s in range(micro)]
        halves = []
        for s in range(micro):
            mixed = lower[s][0]
            other = lax.ppermute(
                lax.dynamic_index_in_dim(mixed, 1 - mp, 0, keepdims=False), "mp", mp_swap
            )
            own = lax.dynamic_index_in_dim(mixed, mp, 0, keepdims=False)
            base = lax.dynamic_index_in_dim(incoming[s], mp, 0, keepdims=False)
            low = (base.astype(F32) + (own.astype(F32) + other.astype(F32))).astype(BF16)
            halves.append(jnp.where(seg == 1, upper_half[s], low))
        sections = jnp.concatenate(halves, axis=0)[None]

        kg = jnp.concatenate([jnp.where(seg == 1, upper[s][1], lower[s][1]) for s in range(micro)], 0)
        vg = jnp.concatenate([jnp.where(seg == 1, upper[s][2], lower[s][2]) for s in range(micro)], 0)
        parts = run_encoder(order, kg, vg, wk, wv)
        away = lax.dynamic_slice_in_dim(parts, (1 - seg) * 2, 2, 0)
        mine = lax.dynamic_slice_in_dim(parts, seg * 2, 2, 0)
        arrived = lax.ppermute(away, "segment", mp_swap)
        summed = (mine.astype(F32) + arrived.astype(F32)).astype(BF16)
        crossing = lax.ppermute(
            lax.dynamic_index_in_dim(summed, 1 - mp, 0, keepdims=False), "mp", mp_swap
        )
        kept = lax.dynamic_index_in_dim(summed, mp, 0, keepdims=False)
        kept = (kept.astype(F32) + crossing.astype(F32)).astype(BF16)

    tiles = kept.shape[0] // TILE
    features = kept.shape[1]
    owners = tile_owner.reshape(devices, tiles)
    slot_ids = jnp.arange(CAP, dtype=jnp.int32)[:, None]
    tile_ids = jnp.arange(tiles, dtype=jnp.int32)

    def plan(source):
        source = source % devices
        row = lax.dynamic_index_in_dim(owners, source, 0, keepdims=False)
        return (row // tiles - source + devices) % devices, row % tiles

    def ranks_of(marked):
        return (ranked(marked)[None, :] == slot_ids) & marked[None, :]

    step, slot = plan(me)
    left_step, left_slot = plan(me - 1 + devices)
    right_step, right_slot = plan(me + 1)
    send_left = jnp.sum(jnp.where(ranks_of(step == devices - 1), tile_ids[None, :], 0), axis=1)
    send_right = jnp.sum(jnp.where(ranks_of(step == 1), tile_ids[None, :], 0), axis=1)
    left_hit = ranks_of(left_step == 1)
    right_hit = ranks_of(right_step == devices - 1)
    target = jnp.concatenate(
        [
            jnp.sum(jnp.where(left_hit, left_slot[None, :], 0), axis=1),
            slot,
            jnp.sum(jnp.where(right_hit, right_slot[None, :], 0), axis=1),
        ]
    )
    usable = jnp.concatenate([jnp.any(left_hit, axis=1), step == 0, jnp.any(right_hit, axis=1)])
    chosen = (tile_ids[:, None] == target[None, :]) & usable[None, :]
    candidate_ids = jnp.arange(target.shape[0], dtype=jnp.int32)
    take = jnp.sum(jnp.where(chosen, candidate_ids[None, :], 0), axis=1)

    tiled = (tiles, TILE, features)
    shape = jax.ShapeDtypeStruct(tiled, BF16)
    handed = jax.ShapeDtypeStruct((CAP, TILE, features), BF16)
    local = kept.reshape(tiled)
    to_left, to_right = small_call(
        pick_kernel, jnp.concatenate([send_left, send_right]), [local], [handed, handed]
    )
    forward = [(i, (i + 1) % devices) for i in range(devices)]
    backward = [(b, a) for a, b in forward]
    from_left = lax.ppermute(to_right, "dp", forward)
    from_right = lax.ppermute(to_left, "dp", backward)
    owned = small_call(place_kernel, take, [from_left, local, from_right], shape)
    return sections, owned.reshape(tiles * TILE, features)


def solution(mesh):
    in_specs = (
        P("dp", None),
        P("segment", "dp", "mp"),
        P("segment", "dp", "mp"),
        P("segment", "dp", "mp"),
        P("segment", "mp", "dp"),
        P("segment", "mp", "dp"),
        P("segment", "mp", "dp"),
        P("segment", "mp", "dp"),
        P("dp", None),
        P("dp", None),
        P("dp", None),
        P(),
    )
    out_specs = (P("segment", "dp", "mp"), P("dp", ("segment", "mp")))
    return jax.shard_map(
        on_device, mesh=mesh, in_specs=in_specs, out_specs=out_specs, check_vma=False
    )
```

```python
import functools

import jax
import jax.numpy as jnp
from jax import lax
from jax.experimental import pallas as pl
from jax.experimental.pallas import tpu as pltpu
from jax.sharding import PartitionSpec as P

DH = 256
TILE = 128
CAP = 2
BLOCK = 256
masked_floor = -1e30
BF16, F32 = jnp.bfloat16, jnp.float32


def dot(a, b, ca, cb):
    return lax.dot_general(a, b, (((ca,), (cb,)), ((), ())), preferred_element_type=F32)


def tick_kernel(count, half, sc, g_ref, q_ref, k_ref, v_ref, *rest):
    wo, wq = rest[:count], rest[count : 2 * count]
    mixed_ref, kg_ref, vg_ref, acc = rest[2 * count :]
    head = pl.program_id(0)
    per = half // BLOCK
    scale = DH ** (-0.5)

    def place(b):
        src = sc[b]
        return src // per, pl.ds(pl.multiple_of((src % per) * BLOCK, BLOCK), BLOCK)

    og = None
    for b in range(count):
        at, cols = place(b)
        term = dot(g_ref[at, :, cols], wo[b][...], 1, 1)
        og = term if og is None else og + term
    og = og.astype(BF16)
    q, k, v = q_ref[0], k_ref[0], v_ref[0]
    scores = dot(q, k, 1, 1) * scale
    rows = lax.broadcasted_iota(jnp.int32, scores.shape, 0)
    cols_id = lax.broadcasted_iota(jnp.int32, scores.shape, 1)
    allowed = None
    for e in range(2):
        q_len, k_off, k_len = sc[count + e], sc[count + 2 + e] * TILE, sc[count + 4 + e]
        hit = (rows >= e * TILE) & (rows < e * TILE + q_len)
        hit = hit & (cols_id >= k_off) & (cols_id < k_off + k_len)
        allowed = hit if allowed is None else allowed | hit
    masked = jnp.where(allowed, scores, masked_floor)
    top = jnp.max(masked, axis=-1, keepdims=True)
    terms = jnp.where(allowed, jnp.exp(masked - top), 0.0)
    prob = terms / jnp.maximum(jnp.sum(terms, axis=-1, keepdims=True), 1.0)
    prob_bf = prob.astype(BF16)
    attended = dot(prob_bf, v, 1, 0)
    out_dot = jnp.sum(og.astype(F32) * attended, axis=-1, keepdims=True)
    sg = (prob * (dot(og, v, 1, 1) - out_dot)).astype(BF16)
    qg = (dot(sg, k, 1, 0) * scale).astype(BF16)
    kg_ref[...] = (dot(sg, q, 0, 0) * scale).astype(BF16)
    vg_ref[...] = dot(prob_bf, og, 0, 0).astype(BF16)

    @pl.when(head == 0)
    def _():
        acc[...] = jnp.zeros_like(acc)

    for b in range(count):
        at, cols = place(b)
        acc[at, :, cols] += dot(qg, wq[b][...], 1, 0)

    @pl.when(head == pl.num_programs(0) - 1)
    def _():
        mixed_ref[...] = acc[...].astype(BF16)


def run_tick(scalars, grad, at, seq, saved_q, saved_k, saved_v, wo, wq, q_rows, k_rows):
    half = grad.shape[2]
    heads = saved_q.shape[2] // DH
    count = len(wo)
    weight = pl.BlockSpec((DH, BLOCK), lambda h, sc: (h, 0))
    macs = heads * q_rows * DH * (4 * half + 6 * k_rows)
    return pl.pallas_call(
        functools.partial(tick_kernel, count, half),
        grid_spec=pltpu.PrefetchScalarGridSpec(
            num_scalar_prefetch=1,
            grid=(heads,),
            in_specs=[
                pl.BlockSpec((2, q_rows, half), lambda h, sc: (0, at, 0)),
                pl.BlockSpec((1, q_rows, DH), lambda h, sc: (0, seq, h)),
                pl.BlockSpec((1, k_rows, DH), lambda h, sc: (0, seq, h)),
                pl.BlockSpec((1, k_rows, DH), lambda h, sc: (0, seq, h)),
            ]
            + [weight] * (2 * count),
            out_specs=[
                pl.BlockSpec((2, q_rows, half), lambda h, sc: (0, 0, 0)),
                pl.BlockSpec((k_rows, DH), lambda h, sc: (0, h)),
                pl.BlockSpec((k_rows, DH), lambda h, sc: (0, h)),
            ],
            scratch_shapes=[pltpu.VMEM((2, q_rows, half), F32)],
        ),
        out_shape=[
            jax.ShapeDtypeStruct((2, q_rows, half), BF16),
            jax.ShapeDtypeStruct((k_rows, heads * DH), BF16),
            jax.ShapeDtypeStruct((k_rows, heads * DH), BF16),
        ],
        compiler_params=pltpu.CompilerParams(vmem_limit_bytes=40 << 20),
        cost_estimate=pl.CostEstimate(
            flops=2 * macs, bytes_accessed=16 << 20, transcendentals=heads * q_rows * k_rows
        ),
    )(scalars, grad, saved_q, saved_k, saved_v, *wo, *wq)


def encoder_kernel(count, quarter, sc, kg_ref, vg_ref, *rest):
    wk, wv, out_ref = rest[:count], rest[count : 2 * count], rest[2 * count]
    per = quarter // BLOCK
    kg, vg = kg_ref[...], vg_ref[...]
    for b in range(count):
        src = sc[b]
        cols = pl.ds(pl.multiple_of((src % per) * BLOCK, BLOCK), BLOCK)
        part = dot(kg, wk[b][...], 1, 0) + dot(vg, wv[b][...], 1, 0)
        out_ref[src // per, :, cols] = part.astype(BF16)


def run_encoder(scalars, kg, vg, wk, wv):
    count = len(wk)
    rows, depth = kg.shape
    quarter = count * BLOCK // 4
    step = 256
    whole = pl.BlockSpec((depth, BLOCK), lambda i, sc: (0, 0))
    return pl.pallas_call(
        functools.partial(encoder_kernel, count, quarter),
        grid_spec=pltpu.PrefetchScalarGridSpec(
            num_scalar_prefetch=1,
            grid=(rows // step,),
            in_specs=[pl.BlockSpec((step, depth), lambda i, sc: (i, 0))] * 2
            + [whole] * (2 * count),
            out_specs=pl.BlockSpec((4, step, quarter), lambda i, sc: (0, i, 0)),
        ),
        out_shape=jax.ShapeDtypeStruct((4, rows, quarter), BF16),
        compiler_params=pltpu.CompilerParams(vmem_limit_bytes=48 << 20),
        cost_estimate=pl.CostEstimate(
            flops=16 * rows * depth * quarter, bytes_accessed=14 << 20, transcendentals=0
        ),
    )(scalars, kg, vg, *wk, *wv)


def pick_kernel(sc, local_ref, left_ref, right_ref):
    for c in range(CAP):
        left_ref[c] = local_ref[sc[c]]
        right_ref[c] = local_ref[sc[CAP + c]]


def place_kernel(sc, left_ref, local_ref, right_ref, out_ref):
    tiles = local_ref.shape[0]
    for s in range(tiles):
        i = sc[s]

        @pl.when(i < CAP)
        def _():
            out_ref[s] = left_ref[jnp.minimum(i, CAP - 1)]

        @pl.when((i >= CAP) & (i < CAP + tiles))
        def _():
            out_ref[s] = local_ref[jnp.clip(i - CAP, 0, tiles - 1)]

        @pl.when(i >= CAP + tiles)
        def _():
            out_ref[s] = right_ref[jnp.clip(i - CAP - tiles, 0, CAP - 1)]


def small_call(body, scalars, arrays, outs):
    vmem = pl.BlockSpec(memory_space=pltpu.VMEM)
    single = not isinstance(outs, list)
    return pl.pallas_call(
        body,
        in_specs=[pl.BlockSpec(memory_space=pltpu.SMEM)] + [vmem] * len(arrays),
        out_specs=vmem if single else [vmem] * len(outs),
        out_shape=outs,
        compiler_params=pltpu.CompilerParams(vmem_limit_bytes=24 << 20),
    )(scalars, *arrays)


def gathered(shard):
    full = lax.all_gather(shard, "dp", axis=1, tiled=True)
    blocks = [full[:, i : i + BLOCK] for i in range(0, full.shape[1], BLOCK)]
    return blocks, list(jnp.arange(len(blocks), dtype=jnp.int32))


def fused_kernel(dims, sc, top_ref, q_ref, k_ref, v_ref, wo_ref, wq_ref, wk_ref, wv_ref,
                 sections_ref, local_ref, wbuf, kg, vg, acc, mixed, other, section, incoming,
                 parts, arrived, summed, crossed,
                 zs, zr, xs, xr, ms, mr, ss, sr, es, er, ps, pr, ys, yr):
    q_rows, k_rows, outer, heads = dims
    half = acc.shape[2]
    per = half // BLOCK
    scale = DH ** (-0.5)
    seg, me, mp = lax.axis_index("segment"), lax.axis_index("dp"), lax.axis_index("mp")
    z, x = me // 2, me % 2
    up = ((z + 1) % outer) * 2 + x
    down = ((z + outer - 1) % outer) * 2 + x
    side = z * 2 + 1 - x
    weights = (wo_ref, wq_ref, wk_ref, wv_ref)
    mesh_id = pl.DeviceIdType.MESH

    barrier = pltpu.get_barrier_semaphore()
    for peer in ((seg, up, mp), (seg, down, mp), (seg, side, mp), (seg, me, 1 - mp), (1 - seg, me, mp)):
        pl.semaphore_signal(barrier, inc=1, device_id=peer, device_id_type=mesh_id)
    pl.semaphore_wait(barrier, 5)

    def block(w, r, sx):
        return weights[w].at[0] if r == 0 and sx == 0 else wbuf.at[w, r * 2 + sx]

    def source(r, sx):
        return ((z + outer - r) % outer) * 2 + (x if sx == 0 else 1 - x)

    def send(src, dst, a, b, peer):
        return pltpu.make_async_remote_copy(
            src_ref=src, dst_ref=dst, send_sem=a, recv_sem=b, device_id=peer, device_id_type=mesh_id
        )

    def z_copy(w, r):
        return send(block(w, r, 0), block(w, r + 1, 0), zs.at[w, r], zr.at[w, r], (seg, up, mp))

    last = outer - 1
    depth = kg.shape[1]
    upper_rows, lower_rows = pl.ds(0, depth // 2), pl.ds(depth // 2, depth // 2)

    def x_copy(w, r):
        src, dst = block(w, r, 0), block(w, r, 1)
        if r == last:
            src, dst = src.at[upper_rows], dst.at[upper_rows]
        return send(src, dst, xs.at[w, r], xr.at[w, r], (seg, side, mp))

    def extra_copy(w):
        src, dst = block(w, last - 1, 1).at[lower_rows], block(w, last, 1).at[lower_rows]
        return send(src, dst, es.at[w], er.at[w], (seg, up, mp))

    def extras(pair):
        for w in pair:
            x_copy(w, last - 1).wait_recv()
            extra_copy(w).start()

    def advance(pair, r):
        for w in pair:
            if r > 0:
                z_copy(w, r - 1).wait_recv()
            if r < outer - 1:
                z_copy(w, r).start()
            x_copy(w, r).start()

    def arrive(pair, r):
        for w in pair:
            if r != last - 1:
                x_copy(w, r).wait_recv()
            if r == last:
                extra_copy(w).wait_recv()

    slots = [(r, sx) for r in range(outer) for sx in range(2)]

    def tick(s, grad):
        acc[...] = jnp.zeros_like(acc)

        def one_head(h, carry):
            hs = pl.ds(pl.multiple_of(h * DH, DH), DH)
            og = jnp.zeros((q_rows, DH), F32)
            for r, sx in slots:
                og += dot(grad(source(r, sx)), block(0, r, sx)[hs, :], 1, 1)
            og = og.astype(BF16)
            q = q_ref[0, s * q_rows : (s + 1) * q_rows, hs]
            k = k_ref[0, s * k_rows : (s + 1) * k_rows, hs]
            v = v_ref[0, s * k_rows : (s + 1) * k_rows, hs]
            scores = dot(q, k, 1, 1) * scale
            rows = lax.broadcasted_iota(jnp.int32, scores.shape, 0)
            cols = lax.broadcasted_iota(jnp.int32, scores.shape, 1)
            allowed = None
            for e in range(2):
                q_len, k_off, k_len = sc[s, e], sc[s, 2 + e] * TILE, sc[s, 4 + e]
                hit = (rows >= e * TILE) & (rows < e * TILE + q_len)
                hit = hit & (cols >= k_off) & (cols < k_off + k_len)
                allowed = hit if allowed is None else allowed | hit
            masked = jnp.where(allowed, scores, masked_floor)
            peak = jnp.max(masked, axis=-1, keepdims=True)
            terms = jnp.where(allowed, jnp.exp(masked - peak), 0.0)
            prob = terms / jnp.maximum(jnp.sum(terms, axis=-1, keepdims=True), 1.0)
            prob_bf = prob.astype(BF16)
            attended = dot(prob_bf, v, 1, 0)
            out_dot = jnp.sum(og.astype(F32) * attended, axis=-1, keepdims=True)
            sg = (prob * (dot(og, v, 1, 1) - out_dot)).astype(BF16)
            qg = (dot(sg, k, 1, 0) * scale).astype(BF16)
            kg[s * k_rows : (s + 1) * k_rows, hs] = (dot(sg, q, 0, 0) * scale).astype(BF16)
            vg[s * k_rows : (s + 1) * k_rows, hs] = dot(prob_bf, og, 0, 0).astype(BF16)
            for r, sx in slots:
                src = source(r, sx)
                at = pl.ds(pl.multiple_of((src % per) * BLOCK, BLOCK), BLOCK)
                acc[src // per, :, at] += dot(qg, block(1, r, sx)[hs, :], 1, 0)
            return carry

        lax.fori_loop(0, heads, one_head, 0)
        mixed[s] = acc[...].astype(BF16)

    def top_block(s):
        def load(src):
            at = pl.ds(pl.multiple_of(src * BLOCK, BLOCK), BLOCK)
            return top_ref[s * q_rows : (s + 1) * q_rows, at]

        return load

    def incoming_block(s):
        def load(src):
            at = pl.ds(pl.multiple_of((src % per) * BLOCK, BLOCK), BLOCK)
            return incoming[s, src // per, :, at]

        return load

    def upper_copy(s):
        return send(mixed.at[s], other.at[s], ms.at[0, s], mr.at[0, s], (seg, me, 1 - mp))

    def lower_copy(s):
        return send(mixed.at[s, 1 - mp], other.at[s, 0], ms.at[1, s], mr.at[1, s], (seg, me, 1 - mp))

    def layer_copy(s):
        return send(section.at[s], incoming.at[s], ss.at[s], sr.at[s], (1 - seg, me, mp))

    def finish_upper(s):
        upper_copy(s).wait_recv()
        rows = slice(s * q_rows, (s + 1) * q_rows)
        for i in range(2):
            base = top_ref[rows, i * half : (i + 1) * half].astype(F32)
            total = base + (mixed[s, i].astype(F32) + other[s, i].astype(F32))
            section[s, i] = total.astype(BF16)
        layer_copy(s).start()
        sections_ref[0, rows, :] = section[s, mp]

    def finish_lower(s):
        lower_copy(s).wait_recv()
        rows = slice(s * q_rows, (s + 1) * q_rows)
        total = mixed[s, mp].astype(F32) + other[s, 0].astype(F32)
        sections_ref[0, rows, :] = (incoming[s, mp].astype(F32) + total).astype(BF16)

    for r in range(outer):
        advance((0, 1), r)
    extras((0, 1))
    advance((2, 3), 0)
    for r in range(outer):
        arrive((0, 1), r)

    @pl.when(seg == 1)
    def _():
        tick(0, top_block(0))
        upper_copy(0).start()

    advance((2, 3), 1)

    @pl.when(seg == 1)
    def _():
        tick(1, top_block(1))
        upper_copy(1).start()
        finish_upper(0)

    for r in range(2, outer - 1):
        advance((2, 3), r)

    @pl.when(seg == 1)
    def _():
        finish_upper(1)

    @pl.when(seg == 0)
    def _():
        layer_copy(0).wait_recv()
        tick(0, incoming_block(0))
        lower_copy(0).start()


    @pl.when(seg == 0)
    def _():
        layer_copy(1).wait_recv()
        tick(1, incoming_block(1))
        lower_copy(1).start()
        finish_lower(0)

    advance((2, 3), last)
    step = 256

    def quarter_of(r):
        return (z + outer - r) % outer

    def part_copy(r):
        q = quarter_of(r)
        return send(parts.at[q], arrived.at[q % 2], ps.at[r], pr.at[r], (1 - seg, me, mp))

    def cross_copy(r):
        return send(summed.at[quarter_of(r) % 2], crossed, ys.at[0], yr.at[0], (seg, me, 1 - mp))

    def encode(r):
        q = quarter_of(r)

        def rows_step(i, carry):
            rows = pl.ds(pl.multiple_of(i * step, step), step)
            for sx in range(2):
                at = pl.ds(pl.multiple_of((x if sx == 0 else 1 - x) * BLOCK, BLOCK), BLOCK)
                part = dot(kg[rows, :], block(2, r, sx)[...], 1, 0)
                part += dot(vg[rows, :], block(3, r, sx)[...], 1, 0)
                parts[q, rows, at] = part.astype(BF16)
            return carry

        lax.fori_loop(0, kg.shape[0] // step, rows_step, 0)

        @pl.when(seg != q // 2)
        def _():
            part_copy(r).start()

    def reduce(r):
        q = quarter_of(r)

        @pl.when(seg == q // 2)
        def _():
            part_copy(r).wait_recv()
            summed[q % 2] = (parts[q].astype(F32) + arrived[q % 2].astype(F32)).astype(BF16)

            @pl.when(mp != q % 2)
            def _():
                cross_copy(r).start()

    for r in range(outer):
        if r == last:

            @pl.when(seg == 0)
            def _():
                finish_lower(1)

        arrive((2, 3), r)
        encode(r)
        if r == 0:
            extras((2, 3))
        else:
            reduce(r - 1)
    reduce(last)
    cross_copy(0).wait_recv()
    local_ref[...] = (summed[mp].astype(F32) + crossed[...].astype(F32)).astype(BF16)
    cross_copy(0).wait_send()
    for r in range(outer):

        @pl.when(seg != quarter_of(r) // 2)
        def _():
            part_copy(r).wait_send()

    @pl.when(seg == 0)
    def _():
        for s in range(2):
            lower_copy(s).wait_send()

    @pl.when(seg == 1)
    def _():
        for s in range(2):
            upper_copy(s).wait_send()
            layer_copy(s).wait_send()

    for w in range(4):
        for r in range(outer):
            x_copy(w, r).wait_send()
            if r == last:
                extra_copy(w).wait_send()
            if r < outer - 1:
                z_copy(w, r).wait_send()


def run_fused(scalars, top, q, k, v, wo, wq, wk, wv, outer):
    micro = scalars.shape[0]
    q_rows, k_rows = top.shape[0] // micro, k.shape[1] // micro
    width, depth = top.shape[1], q.shape[2]
    half = width // 2
    vmem = pl.BlockSpec(memory_space=pltpu.VMEM)
    dma = pltpu.SemaphoreType.DMA
    return pl.pallas_call(
        functools.partial(fused_kernel, (q_rows, k_rows, outer, depth // DH)),
        in_specs=[pl.BlockSpec(memory_space=pltpu.SMEM)] + [vmem] * 8,
        out_specs=[vmem, vmem],
        out_shape=[
            jax.ShapeDtypeStruct((1, micro * q_rows, half), BF16),
            jax.ShapeDtypeStruct((micro * k_rows, width // 4), BF16),
        ],
        scratch_shapes=[
            pltpu.VMEM((4, 2 * outer, depth, BLOCK), BF16),
            pltpu.VMEM((micro * k_rows, depth), BF16),
            pltpu.VMEM((micro * k_rows, depth), BF16),
            pltpu.VMEM((2, q_rows, half), F32),
        ]
        + [pltpu.VMEM((micro, 2, q_rows, half), BF16)] * 4
        + [pltpu.VMEM((n, micro * k_rows, width // 4), BF16) for n in (4, 2, 2)]
        + [pltpu.VMEM((micro * k_rows, width // 4), BF16)]
        + [dma((4, outer))] * 4
        + [dma((2, micro))] * 2
        + [dma((micro,))] * 2
        + [dma((4,))] * 2
        + [dma((outer,))] * 2
        + [dma((1,))] * 2,
        compiler_params=pltpu.CompilerParams(
            collective_id=0, has_side_effects=True, vmem_limit_bytes=58 << 20
        ),
    )(scalars, top, q, k, v, wo, wq, wk, wv)


def ranked(marked):
    ids = jnp.arange(marked.shape[0], dtype=jnp.int32)
    upto = ids[None, :] <= ids[:, None]
    return jnp.sum((upto & marked[None, :]).astype(jnp.int32), axis=1) - 1


def on_device(
    grad_top,
    saved_query,
    saved_key,
    saved_value,
    w_query,
    w_key,
    w_value,
    w_out,
    query_length,
    key_offset,
    key_length,
    tile_owner,
):
    seg = lax.axis_index("segment")
    mp = lax.axis_index("mp")
    devices = lax.axis_size("dp")
    me = lax.axis_index("dp")
    micro = query_length.shape[0]
    q_rows = grad_top.shape[0] // micro
    k_rows = saved_key.shape[1] // micro
    half = grad_top.shape[1] // 2
    mp_swap = [(0, 1), (1, 0)]
    if w_out.shape[2] == BLOCK and devices == 8 and micro == 2:
        table = jnp.concatenate([query_length, key_offset, key_length], axis=1)
        sections, kept = run_fused(
            table, grad_top, saved_query, saved_key, saved_value, w_out, w_query, w_key, w_value,
            devices // 2,
        )
    else:
        wo, sources = gathered(w_out[0])
        wq, _ = gathered(w_query[0])
        wk, _ = gathered(w_key[0])
        wv, _ = gathered(w_value[0])
        order = jnp.stack(sources).astype(jnp.int32)

        top = grad_top.reshape(grad_top.shape[0], 2, half).transpose(1, 0, 2)
        scalars = [
            jnp.concatenate([order, query_length[s], key_offset[s], key_length[s]])
            for s in range(micro)
        ]

        def tick(s, grad, at):
            return run_tick(
                scalars[s], grad, at, s, saved_query, saved_key, saved_value, wo, wq, q_rows, k_rows
            )

        upper = [tick(s, top, s) for s in range(micro)]
        upper_half, incoming = [], []
        for s in range(micro):
            mixed = upper[s][0]
            other = lax.ppermute(mixed, "mp", mp_swap)
            rows = top[:, s * q_rows : (s + 1) * q_rows]
            section = (rows.astype(F32) + (mixed.astype(F32) + other.astype(F32))).astype(BF16)
            incoming.append(lax.ppermute(section, "segment", [(1, 0)]))
            upper_half.append(lax.dynamic_index_in_dim(section, mp, 0, keepdims=False))
        lower = [tick(s, incoming[s], 0) for s in range(micro)]
        halves = []
        for s in range(micro):
            mixed = lower[s][0]
            other = lax.ppermute(
                lax.dynamic_index_in_dim(mixed, 1 - mp, 0, keepdims=False), "mp", mp_swap
            )
            own = lax.dynamic_index_in_dim(mixed, mp, 0, keepdims=False)
            base = lax.dynamic_index_in_dim(incoming[s], mp, 0, keepdims=False)
            low = (base.astype(F32) + (own.astype(F32) + other.astype(F32))).astype(BF16)
            halves.append(jnp.where(seg == 1, upper_half[s], low))
        sections = jnp.concatenate(halves, axis=0)[None]

        kg = jnp.concatenate([jnp.where(seg == 1, upper[s][1], lower[s][1]) for s in range(micro)], 0)
        vg = jnp.concatenate([jnp.where(seg == 1, upper[s][2], lower[s][2]) for s in range(micro)], 0)
        parts = run_encoder(order, kg, vg, wk, wv)
        away = lax.dynamic_slice_in_dim(parts, (1 - seg) * 2, 2, 0)
        mine = lax.dynamic_slice_in_dim(parts, seg * 2, 2, 0)
        arrived = lax.ppermute(away, "segment", mp_swap)
        summed = (mine.astype(F32) + arrived.astype(F32)).astype(BF16)
        crossing = lax.ppermute(
            lax.dynamic_index_in_dim(summed, 1 - mp, 0, keepdims=False), "mp", mp_swap
        )
        kept = lax.dynamic_index_in_dim(summed, mp, 0, keepdims=False)
        kept = (kept.astype(F32) + crossing.astype(F32)).astype(BF16)

    tiles = kept.shape[0] // TILE
    features = kept.shape[1]
    owners = tile_owner.reshape(devices, tiles)
    slot_ids = jnp.arange(CAP, dtype=jnp.int32)[:, None]
    tile_ids = jnp.arange(tiles, dtype=jnp.int32)

    def plan(source):
        source = source % devices
        row = lax.dynamic_index_in_dim(owners, source, 0, keepdims=False)
        return (row // tiles - source + devices) % devices, row % tiles

    def ranks_of(marked):
        return (ranked(marked)[None, :] == slot_ids) & marked[None, :]

    step, slot = plan(me)
    left_step, left_slot = plan(me - 1 + devices)
    right_step, right_slot = plan(me + 1)
    send_left = jnp.sum(jnp.where(ranks_of(step == devices - 1), tile_ids[None, :], 0), axis=1)
    send_right = jnp.sum(jnp.where(ranks_of(step == 1), tile_ids[None, :], 0), axis=1)
    left_hit = ranks_of(left_step == 1)
    right_hit = ranks_of(right_step == devices - 1)
    target = jnp.concatenate(
        [
            jnp.sum(jnp.where(left_hit, left_slot[None, :], 0), axis=1),
            slot,
            jnp.sum(jnp.where(right_hit, right_slot[None, :], 0), axis=1),
        ]
    )
    usable = jnp.concatenate([jnp.any(left_hit, axis=1), step == 0, jnp.any(right_hit, axis=1)])
    chosen = (tile_ids[:, None] == target[None, :]) & usable[None, :]
    candidate_ids = jnp.arange(target.shape[0], dtype=jnp.int32)
    take = jnp.sum(jnp.where(chosen, candidate_ids[None, :], 0), axis=1)

    tiled = (tiles, TILE, features)
    shape = jax.ShapeDtypeStruct(tiled, BF16)
    handed = jax.ShapeDtypeStruct((CAP, TILE, features), BF16)
    local = kept.reshape(tiled)
    to_left, to_right = small_call(
        pick_kernel, jnp.concatenate([send_left, send_right]), [local], [handed, handed]
    )
    forward = [(i, (i + 1) % devices) for i in range(devices)]
    backward = [(b, a) for a, b in forward]
    from_left = lax.ppermute(to_right, "dp", forward)
    from_right = lax.ppermute(to_left, "dp", backward)
    owned = small_call(place_kernel, take, [from_left, local, from_right], shape)
    return sections, owned.reshape(tiles * TILE, features)


def solution(mesh):
    in_specs = (
        P("dp", None),
        P("segment", "dp", "mp"),
        P("segment", "dp", "mp"),
        P("segment", "dp", "mp"),
        P("segment", "mp", "dp"),
        P("segment", "mp", "dp"),
        P("segment", "mp", "dp"),
        P("segment", "mp", "dp"),
        P("dp", None),
        P("dp", None),
        P("dp", None),
        P(),
    )
    out_specs = (P("segment", "dp", "mp"), P("dp", ("segment", "mp")))
    return jax.shard_map(
        on_device, mesh=mesh, in_specs=in_specs, out_specs=out_specs, check_vma=False
    )
```
